256 devices in a mesh: slab: 32 (over y_hi, z, core), plane: 8 (over x, y_lo).
Axes of the slice: x: 4, y: 4 (y_hi: 2, y_lo: 2; y = y_hi * 2 + y_lo), z: 8, core: 2. Of those that a mesh axis runs over, the one named last changes fastest.
Arguments:
- features: bfloat16 [32768, 512], P(('slab', 'plane')), may hold values from -6 to 6
- gain: float32 [512], replicated, may hold values from 0.5 to 1.5
- w_query: bfloat16 [512, 512], replicated, may hold values from -0.25 to 0.25
- w_key: bfloat16 [512, 512], replicated, may hold values from -0.25 to 0.25
- w_value: bfloat16 [512, 512], replicated, may hold values from -0.25 to 0.25
- w_out: bfloat16 [512, 512], replicated, may hold values from -0.25 to 0.25
- w_face: bfloat16 [512, 512], replicated, may hold values from -0.25 to 0.25
- gamma: float32 [8], replicated, may hold values from 0.02 to 1
- positions: bfloat16 [3, 32768], P(None, ('slab', 'plane')), may hold values from 0 to 1
- key_bias: bfloat16 [8, 32768], P(None, ('slab', 'plane')), may hold values from -9 to 300
- block_mask: int32 [8, 32, 32], P('plane', 'slab'), may hold values from 0 to 1, as said below
- send_list: int32 [2, 32768], P(None, ('slab', 'plane')), may hold values from 0 to 127, as said below
- neighbour: int32 [32768], P(('slab', 'plane')), may hold values from 0 to 255, as said below
- cotangent: bfloat16 [32768, 512], P(('slab', 'plane')), may hold values from -6 to 6
Outputs:
- out: bfloat16 [32768, 512], P(('slab', 'plane'))
- d_input: bfloat16 [32768, 512], P(('slab', 'plane'))
- d_query_w: float32 [512, 512], replicated
- d_key_w: float32 [512, 512], replicated
- d_value_w: float32 [512, 512], replicated
- d_out_w: float32 [512, 512], replicated
- d_face: float32 [512, 512], replicated
The draws below stay inside these ranges and needn't reach their ends.
Inputs may be any that keep to these rules, and one draw needn't show every extreme that they name: block_mask[p, i, j] is 0 unless slab j lies within 3 slabs of slab i around the loop; block_mask[p, i, i] = 1. `send_list`: each device's list 0 and list 1 each hold 128 distinct local atom indices. `neighbour`: ids below 128 index rows of the list received from group p - 1, the others rows of the list from group p + 1.
All inputs are finite; a program needn't handle non-finite values.
Results may differ from the reference program's by a relative error of at most 0.02.
Values may be sent and summed in bfloat16 or wider, within the bound.
No kernel may reach another device: no remote copies, remote signals or barrier semaphores. Data moves between devices by JAX's collectives and lax.ppermute only.
A program may use at most 64 MiB of HBM per device.

```python
import math
import jax
import jax.numpy as jnp
from jax import lax

D = 512
H = 8
BLK = 128
BLK_DEV = 1
BAND = 3
A_DEV = 128
FACE = 128
ATOMS = 32768
N_SLAB = 32
N_PLANE = 8


def draw_key_bias(key, part):
    key = jax.random.fold_in(key, 41)
    values = 1.5 * jax.random.normal(key, (H, ATOMS), jnp.float32)
    values = jnp.clip(values, -9.0, 300.0)
    return values.astype(jnp.bfloat16)


def draw_block_mask(key, part):
    key = jax.random.fold_in(key, 51)
    total = BLK_DEV * N_SLAB
    row_ids = jnp.arange(total)[:, None]
    col_ids = jnp.arange(total)[None, :]
    apart = (col_ids // BLK_DEV - row_ids // BLK_DEV + N_SLAB) % N_SLAB
    apart = jnp.where(apart > N_SLAB // 2, apart - N_SLAB, apart)
    inside = jnp.abs(apart) <= BAND
    level = jax.random.randint(jax.random.fold_in(key, 1), (N_PLANE, N_SLAB), 0, 4)
    level_rows = jnp.repeat(level, BLK_DEV, axis=1)[:, :, None]
    coins = jax.random.randint(jax.random.fold_in(key, 2), (N_PLANE, total, total), 0, 8)
    keep = coins < 2 + 2 * level_rows
    edge = (jnp.abs(apart) == BAND) & (row_ids % BLK_DEV == 0) & (col_ids % BLK_DEV == 0)
    keep = keep | (row_ids == col_ids)[None] | edge[None]
    return (inside[None] & keep).astype(jnp.int32)


def draw_send_list(key, part):
    key = jax.random.fold_in(key, 61)
    keys = jax.random.split(key, 2 * N_SLAB * N_PLANE)
    orders = jax.vmap(lambda sub: jax.random.permutation(sub, A_DEV))(keys)
    return orders.reshape(2, N_SLAB * N_PLANE * FACE).astype(jnp.int32)


def face_counts(key):
    blocks = jax.random.randint(key, (N_SLAB, N_PLANE, 2), 1, FACE // BLK + 1)
    blocks = blocks.at[0, 1 % N_PLANE, 0].set(FACE // BLK)
    return blocks * BLK


def draw_neighbour(key, part):
    key = jax.random.fold_in(key, 81)
    counts = face_counts(jax.random.fold_in(key, 3))
    from_lower = jnp.roll(counts[:, :, 1], 1, axis=1)[:, :, None]
    from_upper = jnp.roll(counts[:, :, 0], -1, axis=1)[:, :, None]
    side = jax.random.randint(jax.random.fold_in(key, 1), (N_SLAB, N_PLANE, A_DEV), 0, 2)
    limit = jnp.where(side == 0, from_lower, from_upper)
    place = jax.random.randint(jax.random.fold_in(key, 2), (N_SLAB, N_PLANE, A_DEV), 0, limit)
    ids = side * FACE + place
    ids = ids.at[0, 0, 0].set(2 * FACE - 1).at[0, 0, 1].set(0)
    return ids.reshape(N_SLAB * N_PLANE * A_DEV).astype(jnp.int32)


def shard_levels(stream_key, extent, cuts, least, high):
    loudness, own = 1.0, jax.random.fold_in(stream_key, 6)
    for position, parts in cuts:
        steps = jnp.exp(jax.random.uniform(jax.random.fold_in(own, position), (parts,), jnp.float32, least / len(cuts), high / len(cuts)))
        loudness = loudness * jnp.repeat(steps, extent[position] // parts).reshape([-1 if axis == position else 1 for axis in range(len(extent))])
    return loudness


def centred(own_key, dims, scale, most, pieces=(), kind=jnp.bfloat16):
    array = scale * jax.random.normal(own_key, dims, jnp.float32)
    if pieces:
        array = array * shard_levels(own_key, dims, pieces, -0.22, 0.18)
    return jnp.clip(array, -most, most).astype(kind)


def setup_inputs(seed: int = 0) -> dict:
    splits = jax.random.split(jax.random.key(seed), 15)
    return {
        "features": centred(splits[0], (ATOMS, D), 1.0, 6.0, ((0, 256),)),
        "gain": jnp.clip(1.0 + 0.1 * jax.random.normal(splits[1], (D,), jnp.float32), 0.5, 1.5),
        "w_query": centred(splits[2], (D, D), D ** -0.5, 0.25),
        "w_key": centred(splits[3], (D, D), D ** -0.5, 0.25),
        "w_value": centred(splits[4], (D, D), D ** -0.5, 0.25),
        "w_out": centred(splits[5], (D, D), D ** -0.5, 0.25),
        "w_face": centred(splits[6], (D, D), D ** -0.5, 0.25),
        "gamma": jnp.clip(jnp.exp(jax.random.uniform(splits[7], (H,), jnp.float32, math.log(0.02), math.log(1.0))), 0.02, 1.0),
        "positions": jnp.clip(1.0 * jax.random.uniform(splits[8], (3, ATOMS), jnp.float32) ** shard_levels(splits[8], (3, ATOMS), ((1, 256),), -0.2, 0.2), 0.0, 1.0).astype(jnp.bfloat16),
        "key_bias": draw_key_bias(jax.random.fold_in(splits[14], 71), 0),
        "block_mask": draw_block_mask(jax.random.fold_in(splits[14], 71), 0),
        "send_list": draw_send_list(jax.random.fold_in(splits[14], 71), 0),
        "neighbour": draw_neighbour(jax.random.fold_in(splits[14], 71), 0),
        "cotangent": centred(splits[13], (ATOMS, D), 1.0, 6.0, ((0, 256),)),
    }


EPS = 1e-06

def softmax_rows(scores):
    highest = lax.optimization_barrier(jnp.max(scores, axis=2, keepdims=True))
    weights = jnp.exp(scores - highest)
    return weights / lax.optimization_barrier(jnp.sum(weights, axis=2, keepdims=True))

def band_scores(query_rows, key_rows, query_pos, key_pos, key_bias, allowed, gamma, scale):
    scores = jnp.einsum('ihd,jhd->hij', query_rows, key_rows) * scale
    span = (query_pos[0][:, None] - key_pos[0][None, :]) ** 2
    span = span + (query_pos[1][:, None] - key_pos[1][None, :]) ** 2
    span = span + (query_pos[2][:, None] - key_pos[2][None, :]) ** 2
    scores = scores + key_bias[:, None, :] - gamma[:, None, None] * span[None]
    return jnp.where(allowed[None], scores, -jnp.inf)

def reference(features, gain, w_query, w_key, w_value, w_out, w_face, gamma, positions, key_bias, block_mask, send_list, neighbour, cotangent):
    width = D // H
    scale = 1.0 / width ** 0.5
    window = 2 * BAND + 1
    units = N_SLAB * N_PLANE
    feat_wide = features.astype(jnp.float32)
    inverse = lax.rsqrt(lax.optimization_barrier(jnp.mean(feat_wide * feat_wide, axis=1, keepdims=True)) + EPS)
    normed = (feat_wide * inverse * gain).astype(jnp.bfloat16)
    query = jnp.dot(normed, w_query, preferred_element_type=jnp.float32).astype(jnp.bfloat16)
    keyed = jnp.dot(normed, w_key, preferred_element_type=jnp.float32).astype(jnp.bfloat16)
    valued = jnp.dot(normed, w_value, preferred_element_type=jnp.float32).astype(jnp.bfloat16)
    query_all = query.reshape(N_SLAB, N_PLANE, A_DEV, H, width)
    key_all = keyed.reshape(N_SLAB, N_PLANE, A_DEV, H, width)
    value_all = valued.reshape(N_SLAB, N_PLANE, A_DEV, H, width)
    pos_all = positions.reshape(3, N_SLAB, N_PLANE, A_DEV)
    bias_all = key_bias.reshape(H, N_SLAB, N_PLANE, A_DEV)
    shifts = jnp.arange(-BAND, BAND + 1, dtype=jnp.int32)

    def context(unit):
        slab = unit // N_PLANE
        plane = unit % N_PLANE
        slab_ids = (slab + shifts) % N_SLAB
        query_rows = query_all[slab, plane].astype(jnp.float32)
        key_rows = key_all[slab_ids, plane].reshape(window * A_DEV, H, width).astype(jnp.float32)
        value_rows = value_all[slab_ids, plane].reshape(window * A_DEV, H, width).astype(jnp.float32)
        query_pos = pos_all[:, slab, plane].astype(jnp.float32)
        near_pos = pos_all[:, slab_ids, plane].astype(jnp.float32)
        lifted = near_pos[2] + shifts.astype(jnp.float32)[:, None]
        key_pos = jnp.stack([near_pos[0], near_pos[1], lifted]).reshape(3, window * A_DEV)
        bias_rows = bias_all[:, slab_ids, plane].reshape(H, window * A_DEV).astype(jnp.float32)
        mask_rows = lax.dynamic_slice(block_mask, (plane, slab * BLK_DEV, jnp.int32(0)), (1, BLK_DEV, BLK_DEV * N_SLAB))[0]
        mask_rows = mask_rows.reshape(BLK_DEV, N_SLAB, BLK_DEV)[:, slab_ids, :].reshape(BLK_DEV, window * BLK_DEV)
        allowed = jnp.repeat(jnp.repeat(mask_rows, BLK, axis=0), BLK, axis=1) > 0
        return (slab, plane, slab_ids, query_rows, key_rows, value_rows, query_pos, key_pos, bias_rows, allowed)

    def forward_unit(unit):
        slab, plane, slab_ids, query_rows, key_rows, value_rows, query_pos, key_pos, bias_rows, allowed = context(unit)
        prob = softmax_rows(band_scores(query_rows, key_rows, query_pos, key_pos, bias_rows, allowed, gamma, scale))
        prob_b = lax.optimization_barrier(prob.astype(jnp.bfloat16)).astype(jnp.float32)
        return jnp.einsum('hij,jhd->ihd', prob_b, value_rows).reshape(A_DEV, D).astype(jnp.bfloat16)
    heads_out = lax.map(forward_unit, jnp.arange(units, dtype=jnp.int32)).reshape(ATOMS, D)
    mixed = (feat_wide + jnp.dot(heads_out, w_out, preferred_element_type=jnp.float32)).astype(jnp.bfloat16)
    mixed_units = mixed.reshape(N_SLAB, N_PLANE, A_DEV, D)
    lists = send_list.reshape(2, N_SLAB, N_PLANE, FACE).transpose(1, 2, 0, 3)
    take_rows = jax.vmap(jax.vmap(lambda rows, picks: rows[picks]))
    sent = take_rows(mixed_units, lists)
    received = jnp.concatenate([jnp.roll(sent[:, :, 1], 1, axis=1), jnp.roll(sent[:, :, 0], -1, axis=1)], axis=2)
    near_ids = neighbour.reshape(N_SLAB, N_PLANE, A_DEV)
    picked = take_rows(received, near_ids).reshape(ATOMS, D)
    out = (mixed.astype(jnp.float32) + jnp.dot(picked, w_face, preferred_element_type=jnp.float32)).astype(jnp.bfloat16)
    d_face = jnp.dot(picked.T, cotangent, preferred_element_type=jnp.float32)
    row_grad = jnp.dot(cotangent, w_face.T, preferred_element_type=jnp.float32).reshape(N_SLAB, N_PLANE, A_DEV, D)
    gather_sums = jax.vmap(jax.vmap(lambda rows, ids: jax.ops.segment_sum(rows, ids, num_segments=2 * FACE)))
    back_rows = gather_sums(row_grad, near_ids).astype(jnp.bfloat16)
    to_down = jnp.roll(back_rows[:, :, FACE:], 1, axis=1).astype(jnp.float32)
    to_up = jnp.roll(back_rows[:, :, :FACE], -1, axis=1).astype(jnp.float32)
    add_rows = jax.vmap(jax.vmap(lambda picks, down, upper: jnp.zeros((A_DEV, D), jnp.float32).at[picks[0]].add(down).at[picks[1]].add(upper)))
    d_mixed = cotangent.astype(jnp.float32) + add_rows(lists, to_down, to_up).reshape(ATOMS, D)
    d_mixed_b = d_mixed.astype(jnp.bfloat16)
    d_out_w = jnp.dot(heads_out.T, d_mixed_b, preferred_element_type=jnp.float32)
    d_heads = jnp.dot(d_mixed_b, w_out.T, preferred_element_type=jnp.float32).astype(jnp.bfloat16)
    heads_all = heads_out.reshape(N_SLAB, N_PLANE, A_DEV, H, width)
    d_heads_all = d_heads.reshape(N_SLAB, N_PLANE, A_DEV, H, width)

    def backward_unit(carry, unit):
        key_sum, value_sum = carry
        slab, plane, slab_ids, query_rows, key_rows, value_rows, query_pos, key_pos, bias_rows, allowed = context(unit)
        d_rows = d_heads_all[slab, plane].astype(jnp.float32)
        delta = lax.optimization_barrier(jnp.sum(d_rows * heads_all[slab, plane].astype(jnp.float32), axis=2)).T
        prob = softmax_rows(band_scores(query_rows, key_rows, query_pos, key_pos, bias_rows, allowed, gamma, scale))
        prob_b = lax.optimization_barrier(prob.astype(jnp.bfloat16)).astype(jnp.float32)
        d_prob = jnp.einsum('ihd,jhd->hij', d_rows, value_rows)
        d_score = prob * (d_prob - delta[:, :, None])
        d_score_b = lax.optimization_barrier(d_score.astype(jnp.bfloat16)).astype(jnp.float32)
        d_query = (jnp.einsum('hij,jhd->ihd', d_score_b, key_rows) * scale).reshape(A_DEV, D)
        d_key = (jnp.einsum('hij,ihd->jhd', d_score_b, query_rows) * scale).reshape(window, A_DEV, D)
        d_value = jnp.einsum('hij,ihd->jhd', prob_b, d_rows).reshape(window, A_DEV, D)
        key_sum = key_sum.at[slab_ids, plane].add(d_key)
        value_sum = value_sum.at[slab_ids, plane].add(d_value)
        return ((key_sum, value_sum), d_query.astype(jnp.bfloat16))
    zeros = jnp.zeros((N_SLAB, N_PLANE, A_DEV, D), jnp.float32)
    sums, d_query = lax.scan(backward_unit, (zeros, zeros), jnp.arange(units, dtype=jnp.int32))
    d_query = d_query.reshape(ATOMS, D)
    d_key = sums[0].reshape(ATOMS, D).astype(jnp.bfloat16)
    d_value = sums[1].reshape(ATOMS, D).astype(jnp.bfloat16)
    d_query_w = jnp.dot(normed.T, d_query, preferred_element_type=jnp.float32)
    d_key_w = jnp.dot(normed.T, d_key, preferred_element_type=jnp.float32)
    d_value_w = jnp.dot(normed.T, d_value, preferred_element_type=jnp.float32)
    d_normed = jnp.dot(d_query, w_query.T, preferred_element_type=jnp.float32)
    d_normed = d_normed + jnp.dot(d_key, w_key.T, preferred_element_type=jnp.float32)
    d_normed = d_normed + jnp.dot(d_value, w_value.T, preferred_element_type=jnp.float32)
    scaled = gain * d_normed
    d_input = (d_mixed + inverse * scaled - feat_wide * inverse ** 3 * lax.optimization_barrier(jnp.mean(scaled * feat_wide, axis=1, keepdims=True))).astype(jnp.bfloat16)
    return (out, d_input, d_query_w, d_key_w, d_value_w, d_out_w, d_face)
```

```python
import jax
import jax.numpy as jnp
from jax import lax
from jax.experimental import pallas as pl
from jax.experimental.pallas import tpu as pltpu
from jax.sharding import PartitionSpec as P

EPS = 1e-06
BF = jnp.bfloat16
F32 = jnp.float32
BOTH = ("slab", "plane")
N = 128
D = 512
HEADS = 8
WINDOW = 7
KEYS = WINDOW * N
VMEM_LIMIT = 50 * 1024 * 1024


def dot(a, b, ca=1, cb=0):
    return lax.dot_general(a, b, (((ca,), (cb,)), ((), ())), preferred_element_type=F32)


def pieces(value):
    high = value.astype(BF).astype(F32)
    rest = value - high
    mid = rest.astype(BF).astype(F32)
    return high, mid, rest - mid


def attend_kernel(
    offs_ref,
    allow_ref,
    gamma_ref,
    half_ref,
    own_ref,
    part_ref,
    low_ref,
    high_ref,
    fwd_ref,
    far_ref,
    cot_ref,
    cot_dn_ref,
    cot_up_ref,
    list_ref,
    gain_ref,
    wq_ref,
    wk_ref,
    wv_ref,
    wo_ref,
    wf_ref,
    keep_ref,
    send_ref,
    sent0_ref,
    sent1_ref,
    mixed_ref,
    dmix_ref,
    dx_own_ref,
    dx_part_ref,
    dx_low_ref,
    dx_high_ref,
    dx_far_ref,
    normed_ref,
    normed_t_ref,
    k_ref,
    v_ref,
    augk_ref,
    augq_ref,
    dk_t_ref,
    dv_t_ref,
    ho_ref,
    dq_ref,
    left_ref,
):
    gain = gain_ref[...]
    blocks = (
        (own_ref, 0),
        (part_ref, 0),
        (low_ref, 0),
        (high_ref, 0),
        (fwd_ref, 0),
        (fwd_ref, 144),
        (far_ref, 0),
    )
    row16 = lax.broadcasted_iota(jnp.int32, (16, N), 0)
    for number, (ref, start) in enumerate(blocks):
        rows = slice(number * N, (number + 1) * N)
        x = ref[start : start + N, :].astype(F32)
        inverse = lax.rsqrt(jnp.mean(x * x, axis=1, keepdims=True) + EPS)
        normed = (x * inverse * gain).astype(BF)
        normed_ref[rows, :] = normed
        normed_t_ref[:, rows] = normed.T
        small = ref[start + N : start + N + 16, 0:N].astype(F32)
        offset = offs_ref[number].astype(F32)
        px, py, pz = small[0:1], small[1:2], small[2:3]
        lifted = pz + offset
        norm2 = px * px + py * py + lifted * lifted
        gam = jnp.concatenate(
            [jnp.full((1, 1), gamma_ref[h], F32) for h in range(HEADS)], axis=0
        )
        bias = small[3:11] - gam * norm2
        bias = jnp.where(allow_ref[number] > 0, bias, -1e30)
        wide = jnp.broadcast_to
        where = jnp.where
        top = where(
            row16 < 3,
            wide(px, (16, N)),
            where(
                row16 < 6,
                wide(py, (16, N)),
                where(row16 < 9, wide(pz, (16, N)), where(row16 < 12, offset, 0.0)),
            ),
        )
        high, mid, low = pieces(bias)
        aug = jnp.concatenate([top, high, mid, low, jnp.zeros((N - 40, N), F32)], axis=0)
        augk_ref[rows, :] = aug.T.astype(BF)
        if number == 0:
            point = where(
                row16 < 3,
                wide(px, (16, N)),
                where(
                    row16 < 6, wide(py, (16, N)), where(row16 < 12, wide(pz, (16, N)), 0.0)
                ),
            )
            row_n = lax.broadcasted_iota(jnp.int32, (N - 16, N), 0)
            for h in range(HEADS):
                high, mid, low = pieces(point * (2.0 * gamma_ref[h]))
                first = where(row16 % 3 == 0, high, where(row16 % 3 == 1, mid, low))
                ones = where(
                    (row_n == h) | (row_n == 8 + h) | (row_n == 16 + h), 1.0, 0.0
                )
                full = jnp.concatenate([first, ones], axis=0)
                augq_ref[h * N : (h + 1) * N, :] = full.T.astype(BF)

    k_ref[...] = dot(normed_ref[...], wk_ref[...]).astype(BF)
    v_ref[...] = dot(normed_ref[...], wv_ref[...]).astype(BF)
    query = (dot(normed_ref[0:N, :], wq_ref[...]).astype(BF) * 0.125).astype(BF)

    row_n = lax.broadcasted_iota(jnp.int32, (N, N), 0)
    list0 = jnp.where(row_n == list_ref[0:1, :], 1.0, 0.0).astype(BF)
    list1 = jnp.where(row_n == list_ref[1:2, :], 1.0, 0.0).astype(BF)
    row_f = row_n.astype(F32)
    near_up = cot_up_ref[N : N + 16, 0:N].astype(F32)[0:1]
    near_dn = cot_dn_ref[N : N + 16, 0:N].astype(F32)[0:1]
    pick_up = jnp.where(row_f == near_up, 1.0, 0.0).astype(BF)
    pick_dn = jnp.where(row_f + 128.0 == near_dn, 1.0, 0.0).astype(BF)
    grad_rows = dot(dot(list1, pick_up).astype(BF), cot_up_ref[0:N, :])
    grad_rows = grad_rows + dot(dot(list0, pick_dn).astype(BF), cot_dn_ref[0:N, :])
    grad_rows = grad_rows.astype(BF)
    d_mixed = cot_ref[...].astype(F32) + dot(grad_rows, wf_ref[...], 1, 1)
    dmix_ref[...] = d_mixed
    d_mixed_b = d_mixed.astype(BF)
    d_heads = dot(d_mixed_b, wo_ref[...], 1, 1).astype(BF)

    lane = lax.broadcasted_iota(jnp.int32, (N, N), 1)
    first = lane < 64
    masks = (first, jnp.logical_not(first))
    masks_b = tuple(jnp.where(m, 1.0, 0.0).astype(BF) for m in masks)
    for pair in range(HEADS // 2):
        cols = slice(pair * N, (pair + 1) * N)
        keys = k_ref[:, cols]
        values = v_ref[:, cols]
        keys_aug = jnp.concatenate([keys, augk_ref[...]], axis=1)
        qp = query[:, cols]
        gp = d_heads[:, cols]
        q_parts = [qp * m for m in masks_b]
        g_parts = [gp * m for m in masks_b]
        probs = []
        probs_b = []
        outs = []
        for t in range(2):
            h = 2 * pair + t
            left = jnp.concatenate([q_parts[t], augq_ref[h * N : (h + 1) * N, :]], axis=1)
            scores = dot(left, keys_aug, 1, 1)
            top = jnp.max(scores, axis=1, keepdims=True)
            weights = jnp.exp(scores - top)
            prob = weights * (1.0 / jnp.sum(weights, axis=1, keepdims=True))
            probs.append(prob)
            probs_b.append(prob.astype(BF))
            outs.append(dot(probs_b[t], values))
        merged = jnp.where(first, outs[0], outs[1]).astype(BF)
        ho_ref[:, cols] = merged
        inner = gp.astype(F32) * merged.astype(F32)
        scores_b = []
        dqs = []
        for t in range(2):
            delta = jnp.sum(jnp.where(masks[t], inner, 0.0), axis=1, keepdims=True)
            d_prob = dot(g_parts[t], values, 1, 1)
            d_score = (probs[t] * (d_prob - delta)).astype(BF)
            scores_b.append(d_score)
            dqs.append(dot(d_score, keys))
        dq_ref[:, cols] = (jnp.where(first, dqs[0], dqs[1]) * 0.125).astype(BF)
        dk_t_ref[cols, :] = dot(
            jnp.concatenate(q_parts, axis=0), jnp.concatenate(scores_b, axis=0), 0, 0
        ).astype(BF)
        dv_t_ref[cols, :] = dot(
            jnp.concatenate(g_parts, axis=0), jnp.concatenate(probs_b, axis=0), 0, 0
        ).astype(BF)

    heads_out = ho_ref[...]
    mixed = (own_ref[0:N, :].astype(F32) + dot(heads_out, wo_ref[...])).astype(BF)
    mixed_ref[...] = mixed
    sent0_ref[...] = dot(list0, mixed, 0, 0).astype(BF)
    sent1_ref[...] = dot(list1, mixed, 0, 0).astype(BF)

    left_ref[0] = heads_out.T
    left_ref[1] = mixed.T
    mine = half_ref[0]
    dq = dq_ref[...]
    for target, side in ((send_ref, 1 - mine), (keep_ref, mine)):
        start = pl.multiple_of(side * 256, 256)
        rows = normed_t_ref[pl.ds(start, 256), :]
        target[0:256, :] = dot(rows[:, 0:N], dq).astype(BF)
        target[256:512, :] = dot(rows, dk_t_ref[...], 1, 1).astype(BF)
        target[512:768, :] = dot(rows, dv_t_ref[...], 1, 1).astype(BF)
        target[768:1024, :] = dot(left_ref[0, pl.ds(start, 256), :], d_mixed_b).astype(BF)
        target[1024:1280, :] = dot(left_ref[1, pl.ds(start, 256), :], grad_rows).astype(BF)

    dx_t = dot(wk_ref[...], dk_t_ref[...]) + dot(wv_ref[...], dv_t_ref[...])
    dx_own_ref[...] = dx_t[:, 0:N] + dot(wq_ref[...], dq, 1, 1)
    dx_part_ref[0] = dx_t[:, N : 2 * N].astype(BF)
    dx_part_ref[1] = dx_t[:, 4 * N : 5 * N].astype(BF)
    dx_part_ref[2] = dx_t[:, 5 * N : 6 * N].astype(BF)
    dx_low_ref[...] = dx_t[:, 2 * N : 3 * N]
    dx_high_ref[...] = dx_t[:, 3 * N : 4 * N]
    dx_far_ref[...] = dx_t[:, 6 * N : 7 * N].astype(BF)


def shape(dims, kind):
    return jax.ShapeDtypeStruct(dims, kind)


def call(kernel, outs, scratch=(), smem=0, flops=1000000):
    def run(*args):
        specs = [
            pl.BlockSpec(memory_space=pltpu.SMEM if number < smem else pltpu.VMEM)
            for number in range(len(args))
        ]
        return pl.pallas_call(
            kernel,
            out_shape=outs,
            in_specs=specs,
            out_specs=jax.tree.map(lambda _: pl.BlockSpec(memory_space=pltpu.VMEM), outs),
            scratch_shapes=list(scratch),
            compiler_params=pltpu.CompilerParams(vmem_limit_bytes=VMEM_LIMIT),
            cost_estimate=pl.CostEstimate(
                flops=flops, bytes_accessed=4000000, transcendentals=0
            ),
        )(*args)

    return run


def split_kernel(place_ref, keep_ref, recv_ref, *outs):
    for half in range(2):
        for step in range(4):
            chunk = lax.rem(place_ref[half] + step, 4)
            rows = pl.ds(pl.multiple_of(half * 640 + chunk * 160, 32), 160)
            total = keep_ref[rows, :].astype(F32) + recv_ref[rows, :].astype(F32)
            out = outs[half * 4 + step]
            out[...] = total.astype(out.dtype)


def resplit_kernel(place_ref, *refs):
    ins, outs, total = refs[:8], refs[8:16], refs[16]
    for half in range(2):
        value = ins[half * 4][...]
        for step in range(1, 4):
            value = value + ins[half * 4 + step][...].astype(F32)
        total[...] = value
        for step in range(4):
            chunk = lax.rem(place_ref[1 - half] + step, 4)
            out = outs[half * 4 + step]
            out[...] = total[pl.ds(pl.multiple_of(chunk * 40, 8), 40), :].astype(out.dtype)


def join_kernel(*refs):
    ins, out, total = refs[:8], refs[8], refs[9]
    for half in range(2):
        value = ins[half * 4][...]
        for step in range(1, 4):
            value = value + ins[half * 4 + step][...].astype(F32)
        total[half * 40 : (half + 1) * 40, :] = value
    out[...] = total[...].astype(BF)


def pair_kernel(a_ref, b_ref, out_ref):
    out_ref[...] = (a_ref[...].astype(F32) + b_ref[...].astype(F32)).astype(BF)


def finish_kernel(place_ref, mine_a, mine_b, other_a, other_b, *refs):
    outs, total = refs[:5], refs[5]
    for whose, (part_a, part_b) in enumerate(((mine_a, mine_b), (other_a, other_b))):
        for half, part in enumerate((part_a, part_b)):
            for big in range(4):
                for little in range(4):
                    outer = lax.rem(place_ref[half] + 4 - big, 4)
                    inner = lax.rem(place_ref[1 - half] + 4 - little, 4)
                    start = pl.multiple_of(half * 640 + outer * 160 + inner * 40, 8)
                    total[whose, pl.ds(start, 40), :] = part[4 * big + little].astype(F32)
    mine = place_ref[2]
    for whose in range(2):
        side = mine if whose == 0 else 1 - mine
        for number in range(5):
            rows = pl.ds(pl.multiple_of(side * 256, 256), 256)
            outs[number][rows, :] = total[whose, number * 256 : (number + 1) * 256, :]


def out_kernel(near_ref, low_ref, high_ref, mixed_ref, wf_ref, out_ref):
    row = lax.broadcasted_iota(jnp.int32, (2 * N, N), 0)
    pick = jnp.where(row == near_ref[...], 1.0, 0.0).astype(BF)
    received = jnp.concatenate([low_ref[...], high_ref[...]], axis=0)
    picked = dot(pick, received, 0, 0).astype(BF)
    out_ref[...] = (mixed_ref[...].astype(F32) + dot(picked, wf_ref[...])).astype(BF)


def add_kernel(low_ref, high_ref, recv_ref, to_low_ref, to_high_ref):
    to_low_ref[...] = (low_ref[...] + recv_ref[1].astype(F32)).astype(BF)
    to_high_ref[...] = (high_ref[...] + recv_ref[2].astype(F32)).astype(BF)


def input_kernel(own_ref, recv_ref, a_ref, b_ref, far_ref, dmix_ref, x_ref, gain_ref, out_ref):
    total = own_ref[...] + recv_ref[0].astype(F32) + a_ref[...].astype(F32)
    total = total + b_ref[...].astype(F32) + far_ref[...].astype(F32)
    scaled = gain_ref[...] * total.T
    x = x_ref[...].astype(F32)
    inverse = lax.rsqrt(jnp.mean(x * x, axis=1, keepdims=True) + EPS)
    drop = x * (inverse * inverse * inverse) * jnp.mean(scaled * x, axis=1, keepdims=True)
    out_ref[...] = (dmix_ref[...] + inverse * scaled - drop).astype(BF)


def device_order(slabs, planes, move):
    rings = slabs // 4
    pairs = []
    for s in range(slabs):
        for p in range(planes):
            c, z, y_hi = s % 2, (s // 2) % rings, s // (2 * rings)
            x, y_lo = p // 2, p % 2
            z2, x2, y2 = move(z, x, 2 * y_hi + y_lo)
            y2 = y2 % 4
            s2 = ((y2 // 2) * rings + z2 % rings) * 2 + c
            pairs.append((s * planes + p, s2 * planes + (x2 % (planes // 2)) * 2 + y2 % 2))
    return pairs


def local(
    features,
    gain,
    w_query,
    w_key,
    w_value,
    w_out,
    w_face,
    gamma,
    positions,
    key_bias,
    block_mask,
    send_list,
    neighbour,
    cotangent,
):
    slabs, planes = lax.axis_size("slab"), lax.axis_size("plane")
    chips = slabs // 2
    slab, plane = lax.axis_index("slab"), lax.axis_index("plane")
    core = slab % 2
    rings = slabs // 4
    x_at, y_at = plane // 2, (slab // (2 * rings)) * 2 + plane % 2

    def along(value, axis, target):
        return lax.ppermute(value, axis, [(i, target(i)) for i in range(lax.axis_size(axis))])

    def chip_step(value, steps):
        return along(value, "slab", lambda s: (s + 2 * steps) % slabs)

    def partner(value):
        return along(value, "slab", lambda s: s ^ 1)

    def far_pair(value):
        return along(value, "slab", lambda s: (s + 3) % slabs if s % 2 else (s - 3) % slabs)

    def plane_step(value, steps):
        return along(value, "plane", lambda p: (p + steps) % planes)

    def x_step(value, k):
        pairs = device_order(slabs, planes, lambda z, x, y: (z, x + k, y))
        return lax.ppermute(value, BOTH, pairs)

    def y_step(value, k):
        pairs = device_order(slabs, planes, lambda z, x, y: (z, x, y + k))
        return lax.ppermute(value, BOTH, pairs)

    def z_flip(value, k):
        pairs = device_order(slabs, planes, lambda z, x, y: (z ^ k, x, y))
        return lax.ppermute(value, BOTH, pairs)

    small = jnp.concatenate([positions, key_bias], axis=0)
    pack = jnp.concatenate([features, jnp.pad(small, ((0, 5), (0, D - N)))], axis=0)
    face_pack = jnp.concatenate(
        [cotangent, jnp.pad(neighbour.astype(BF)[None], ((0, 15), (0, D - N)))], axis=0
    )
    low = chip_step(pack, 1)
    high = chip_step(pack, -1)
    far = far_pair(pack)
    part = partner(pack)
    cot_dn = plane_step(face_pack, 1)
    cot_up = plane_step(face_pack, -1)
    fwd = partner(jnp.concatenate([low, high], axis=0))

    side = 1 - 2 * core
    offsets = jnp.stack(
        [0 * core, side, 0 * core - 2, 0 * core + 2, -1 - 2 * core, 3 - 2 * core, -3 * side]
    ).astype(jnp.int32)
    allow = block_mask[0, 0][(slab + offsets) % slabs]

    results = call(
        attend_kernel,
        (
            shape((1280, D), BF),
            shape((1280, D), BF),
            shape((N, D), BF),
            shape((N, D), BF),
            shape((N, D), BF),
            shape((N, D), F32),
            shape((D, N), F32),
            shape((3, D, N), BF),
            shape((D, N), F32),
            shape((D, N), F32),
            shape((D, N), BF),
        ),
        scratch=(
            pltpu.VMEM((KEYS, D), BF),
            pltpu.VMEM((D, KEYS), BF),
            pltpu.VMEM((KEYS, D), BF),
            pltpu.VMEM((KEYS, D), BF),
            pltpu.VMEM((KEYS, N), BF),
            pltpu.VMEM((HEADS * N, N), BF),
            pltpu.VMEM((D, KEYS), BF),
            pltpu.VMEM((D, KEYS), BF),
            pltpu.VMEM((N, D), BF),
            pltpu.VMEM((N, D), BF),
            pltpu.VMEM((2, D, N), BF),
        ),
        smem=4,
        flops=6000000000,
    )(
        offsets,
        allow,
        gamma,
        core[None],
        pack,
        part,
        low,
        high,
        fwd,
        far,
        cotangent,
        cot_dn,
        cot_up,
        send_list,
        gain[None],
        w_query,
        w_key,
        w_value,
        w_out,
        w_face,
    )
    keep, send, sent0, sent1, mixed, d_mixed, dx_own, dx_part, dx_low, dx_high, dx_far = results

    place = jnp.stack([x_at, y_at, core]).astype(jnp.int32)
    steps = (1, 2, 3)
    got = partner(send)
    chunk = shape((160, D), BF)
    first = call(
        split_kernel,
        (shape((160, D), F32), chunk, chunk, chunk) * 2,
        smem=1,
    )(place, keep, got)
    got_a = [x_step(first[k], k) for k in steps]
    got_b = [y_step(first[4 + k], k) for k in steps]
    chunk = shape((40, D), BF)
    second = call(
        resplit_kernel,
        (shape((40, D), F32), chunk, chunk, chunk) * 2,
        scratch=(pltpu.VMEM((160, D), F32),),
        smem=1,
    )(place, first[0], *got_a, first[4], *got_b)
    got_a = [y_step(second[k], k) for k in steps]
    got_b = [x_step(second[4 + k], k) for k in steps]
    total = call(join_kernel, shape((80, D), BF), scratch=(pltpu.VMEM((80, D), F32),))(second[0], *got_a, second[4], *got_b)
    for k in (1, 2, 4):
        total = call(pair_kernel, shape((80, D), BF))(total, z_flip(total, k))
    own_a, own_b = total[:40], total[40:]
    part_a = jnp.stack([own_a] + [y_step(own_a, k) for k in steps])
    part_b = jnp.stack([own_b] + [x_step(own_b, k) for k in steps])
    half_a = jnp.concatenate([part_a] + [x_step(part_a, k) for k in steps], axis=0)
    half_b = jnp.concatenate([part_b] + [y_step(part_b, k) for k in steps], axis=0)
    other_a, other_b = partner((half_a, half_b))
    weights = call(
        finish_kernel,
        (shape((D, D), F32),) * 5,
        scratch=(pltpu.VMEM((2, 1280, D), F32),),
        smem=1,
    )(place, half_a, half_b, other_a, other_b)

    face_low = plane_step(sent1, 1)
    face_high = plane_step(sent0, -1)
    out = call(out_kernel, shape((N, D), BF))(
        neighbour[None], face_low, face_high, mixed, w_face
    )

    back = partner(dx_part)
    back_far = far_pair(dx_far)
    to_low, to_high = call(add_kernel, (shape((D, N), BF),) * 2)(dx_low, dx_high, back)
    back_a = chip_step(to_low, -1)
    back_b = chip_step(to_high, 1)
    d_input = call(input_kernel, shape((N, D), BF))(
        dx_own, back, back_a, back_b, back_far, d_mixed, features, gain[None]
    )
    return (out, d_input, *weights)


def solution(mesh):
    rows = P(BOTH, None)
    return jax.shard_map(
        local,
        mesh=mesh,
        in_specs=(
            rows,
            P(),
            P(),
            P(),
            P(),
            P(),
            P(),
            P(),
            P(None, BOTH),
            P(None, BOTH),
            P("plane", "slab", None),
            P(None, BOTH),
            P(BOTH),
            rows,
        ),
        out_specs=(rows, rows, P(), P(), P(), P(), P()),
        check_vma=False,
    )
```

```python
import functools

import jax
import jax.numpy as jnp
from jax import lax
from jax.experimental import pallas as pl
from jax.experimental.pallas import tpu as pltpu
from jax.sharding import PartitionSpec as P

EPS = 1e-06
BF = jnp.bfloat16
F32 = jnp.float32
BOTH = ("slab", "plane")
N = 128
D = 512
HEADS = 8
WINDOW = 7
KEYS = WINDOW * N


def dot(a, b, ca=1, cb=0):
    return lax.dot_general(a, b, (((ca,), (cb,)), ((), ())), preferred_element_type=F32)


def pieces(value):
    high = value.astype(BF).astype(F32)
    rest = value - high
    mid = rest.astype(BF).astype(F32)
    return high, mid, rest - mid


def half_grads(stage, target, sems, start, normed_t, dk_t, dv_t, left, dq, d_mixed_b, grad_rows):
    copies = []
    rows = normed_t[pl.ds(start, 256), :]
    for number in range(5):
        if number == 0:
            grad = dot(left[0, pl.ds(start, 256), :], d_mixed_b)
        elif number == 1:
            grad = dot(left[1, pl.ds(start, 256), :], grad_rows)
        elif number == 2:
            grad = dot(rows[:, 0:N], dq)
        else:
            grad = dot(rows, (dk_t if number == 3 else dv_t)[...], 1, 1)
        grad = grad.astype(BF)
        part = slice(number * 16, (number + 1) * 16)
        for chunk in range(16):
            stage[chunk, part, :] = grad[chunk * 16 : (chunk + 1) * 16]
        copy = pltpu.make_async_copy(stage.at[:, part, :], target.at[:, part, :], sems.at[number])
        copy.start()
        copies.append(copy)
    return copies


def attend_kernel(
    offs_ref,
    allow_ref,
    gamma_ref,
    half_ref,
    own_ref,
    near1_ref,
    near2_ref,
    near3_ref,
    fwd0_ref,
    fwd1_ref,
    fwd2_ref,
    cot_ref,
    cot_dn_ref,
    cot_up_ref,
    list_ref,
    gain_ref,
    wk_hbm,
    wv_hbm,
    wq_hbm,
    wf_hbm,
    wo_hbm,
    send_ref,
    keep_ref,
    sent0_ref,
    sent1_ref,
    mixed_ref,
    dmix_ref,
    dx_own_ref,
    dx_part_ref,
    dx_near1_ref,
    dx_near2_ref,
    dx_near3_ref,
    wk_ref,
    wv_ref,
    wq_ref,
    wf_ref,
    wo_ref,
    weight_sems,
    send_stage,
    keep_stage,
    send_sems,
    keep_sems,
    normed_t_ref,
    dk_t_ref,
    dv_t_ref,
    dq_ref,
    left_ref,
    normed_ref,
    k_ref,
    v_ref,
    augk_ref,
    augq_ref,
    ho_ref,
):
    loads = []
    for number, (source, target) in enumerate(
        (
            (wk_hbm, wk_ref),
            (wv_hbm, wv_ref),
            (wq_hbm, wq_ref),
            (wf_hbm, wf_ref),
            (wo_hbm, wo_ref),
        )
    ):
        load = pltpu.make_async_copy(source, target, weight_sems.at[number])
        load.start()
        loads.append(load)
    gain = gain_ref[...]
    blocks = (
        (own_ref, 0),
        (near1_ref, 0),
        (near2_ref, 0),
        (near3_ref, 0),
        (fwd0_ref, 0),
        (fwd1_ref, 0),
        (fwd2_ref, 0),
    )
    row16 = lax.broadcasted_iota(jnp.int32, (16, N), 0)
    for number, (ref, start) in enumerate(blocks):
        rows = slice(number * N, (number + 1) * N)
        x = ref[start : start + N, :].astype(F32)
        inverse = lax.rsqrt(jnp.mean(x * x, axis=1, keepdims=True) + EPS)
        normed = (x * inverse * gain).astype(BF)
        normed_ref[rows, :] = normed
        normed_t_ref[:, rows] = normed.T
        small = ref[start + N : start + N + 16, 0:N].astype(F32)
        offset = offs_ref[number].astype(F32)
        px, py, pz = small[0:1], small[1:2], small[2:3]
        lifted = pz + offset
        norm2 = px * px + py * py + lifted * lifted
        gam = jnp.concatenate(
            [jnp.full((1, 1), gamma_ref[h], F32) for h in range(HEADS)], axis=0
        )
        bias = small[3:11] - gam * norm2
        bias = jnp.where(allow_ref[number] > 0, bias, -1e30)
        wide = jnp.broadcast_to
        where = jnp.where
        top = where(
            row16 < 3,
            wide(px, (16, N)),
            where(
                row16 < 6,
                wide(py, (16, N)),
                where(row16 < 9, wide(pz, (16, N)), where(row16 < 12, offset, 0.0)),
            ),
        )
        high, mid, low = pieces(bias)
        aug = jnp.concatenate([top, high, mid, low, jnp.zeros((N - 40, N), F32)], axis=0)
        augk_ref[rows, :] = aug.T.astype(BF)
        if number == 0:
            point = where(
                row16 < 3,
                wide(px, (16, N)),
                where(
                    row16 < 6, wide(py, (16, N)), where(row16 < 12, wide(pz, (16, N)), 0.0)
                ),
            )
            row_n = lax.broadcasted_iota(jnp.int32, (N - 16, N), 0)
            for h in range(HEADS):
                high, mid, low = pieces(point * (2.0 * gamma_ref[h]))
                first = where(row16 % 3 == 0, high, where(row16 % 3 == 1, mid, low))
                ones = where(
                    (row_n == h) | (row_n == 8 + h) | (row_n == 16 + h), 1.0, 0.0
                )
                full = jnp.concatenate([first, ones], axis=0)
                augq_ref[h * N : (h + 1) * N, :] = full.T.astype(BF)

    for load in loads:
        load.wait()
    k_ref[...] = dot(normed_ref[...], wk_ref[...]).astype(BF)
    v_ref[...] = dot(normed_ref[...], wv_ref[...]).astype(BF)
    query = (dot(normed_ref[0:N, :], wq_ref[...]).astype(BF) * 0.125).astype(BF)

    row_n = lax.broadcasted_iota(jnp.int32, (N, N), 0)
    list0 = jnp.where(row_n == list_ref[0:1, :], 1.0, 0.0).astype(BF)
    list1 = jnp.where(row_n == list_ref[1:2, :], 1.0, 0.0).astype(BF)
    row_f = row_n.astype(F32)
    near_up = cot_up_ref[N : N + 16, 0:N].astype(F32)[0:1]
    near_dn = cot_dn_ref[N : N + 16, 0:N].astype(F32)[0:1]
    pick_up = jnp.where(row_f == near_up, 1.0, 0.0).astype(BF)
    pick_dn = jnp.where(row_f + 128.0 == near_dn, 1.0, 0.0).astype(BF)
    grad_rows = dot(dot(list1, pick_up).astype(BF), cot_up_ref[0:N, :])
    grad_rows = grad_rows + dot(dot(list0, pick_dn).astype(BF), cot_dn_ref[0:N, :])
    grad_rows = grad_rows.astype(BF)
    d_mixed = cot_ref[...].astype(F32) + dot(grad_rows, wf_ref[...], 1, 1)
    dmix_ref[...] = d_mixed
    d_mixed_b = d_mixed.astype(BF)
    d_heads = dot(d_mixed_b, wo_ref[...], 1, 1).astype(BF)

    lane = lax.broadcasted_iota(jnp.int32, (N, N), 1)
    first = lane < 64
    masks = (first, jnp.logical_not(first))
    masks_b = tuple(jnp.where(m, 1.0, 0.0).astype(BF) for m in masks)
    for pair in range(HEADS // 2):
        cols = slice(pair * N, (pair + 1) * N)
        keys = k_ref[:, cols]
        values = v_ref[:, cols]
        keys_aug = jnp.concatenate([keys, augk_ref[...]], axis=1)
        qp = query[:, cols]
        gp = d_heads[:, cols]
        q_parts = [qp * m for m in masks_b]
        g_parts = [gp * m for m in masks_b]
        probs = []
        probs_b = []
        outs = []
        for t in range(2):
            h = 2 * pair + t
            left = jnp.concatenate([q_parts[t], augq_ref[h * N : (h + 1) * N, :]], axis=1)
            scores = dot(left, keys_aug, 1, 1)
            top = jnp.max(scores, axis=1, keepdims=True)
            weights = jnp.exp(scores - top)
            prob = weights * (1.0 / jnp.sum(weights, axis=1, keepdims=True))
            probs.append(prob)
            probs_b.append(prob.astype(BF))
            outs.append(dot(probs_b[t], values))
        merged = jnp.where(first, outs[0], outs[1]).astype(BF)
        ho_ref[:, cols] = merged
        inner = gp.astype(F32) * merged.astype(F32)
        scores_b = []
        dqs = []
        for t in range(2):
            delta = jnp.sum(jnp.where(masks[t], inner, 0.0), axis=1, keepdims=True)
            d_prob = dot(g_parts[t], values, 1, 1)
            d_score = (probs[t] * (d_prob - delta)).astype(BF)
            scores_b.append(d_score)
            dqs.append(dot(d_score, keys))
        dq_ref[:, cols] = (jnp.where(first, dqs[0], dqs[1]) * 0.125).astype(BF)
        dk_t_ref[cols, :] = dot(
            jnp.concatenate(q_parts, axis=0), jnp.concatenate(scores_b, axis=0), 0, 0
        ).astype(BF)
        dv_t_ref[cols, :] = dot(
            jnp.concatenate(g_parts, axis=0), jnp.concatenate(probs_b, axis=0), 0, 0
        ).astype(BF)

    heads_out = ho_ref[...]
    mixed = (own_ref[0:N, :].astype(F32) + dot(heads_out, wo_ref[...])).astype(BF)
    mixed_ref[...] = mixed
    left_ref[0] = heads_out.T
    left_ref[1] = mixed.T
    mine = half_ref[0]
    dq = dq_ref[...]
    copies = []
    for stage, target, sems, side in (
        (send_stage, send_ref, send_sems, 1 - mine),
        (keep_stage, keep_ref, keep_sems, mine),
    ):
        copies += half_grads(
            stage,
            target,
            sems,
            pl.multiple_of(side * 256, 256),
            normed_t_ref,
            dk_t_ref,
            dv_t_ref,
            left_ref,
            dq,
            d_mixed_b,
            grad_rows,
        )

    dx_t = dot(wk_ref[...], dk_t_ref[...]) + dot(wv_ref[...], dv_t_ref[...])
    dx_own_ref[...] = dx_t[:, 0:N] + dot(wq_ref[...], dq, 1, 1)
    dx_near1_ref[...] = dx_t[:, N : 2 * N]
    dx_near2_ref[...] = dx_t[:, 2 * N : 3 * N]
    dx_near3_ref[...] = dx_t[:, 3 * N : 4 * N].astype(BF)
    for number in range(3):
        first = (4 + number) * N
        dx_part_ref[number] = dx_t[:, first : first + N].astype(BF)
    sent0_ref[...] = dot(list0, mixed, 0, 0).astype(BF)
    sent1_ref[...] = dot(list1, mixed, 0, 0).astype(BF)
    for copy in copies:
        copy.wait()


def shape(dims, kind):
    return jax.ShapeDtypeStruct(dims, kind)


def whole(dims):
    return pl.BlockSpec(dims, lambda i: (0,) * len(dims), pipeline_mode=pl.Buffered(1))


def call(kernel, outs, scratch=(), smem=0, flops=1000000, limit=16, far=(), far_out=(), alias=None):
    single = not isinstance(outs, tuple)
    outs = (outs,) if single else outs

    def run(*args):
        hbm = pl.BlockSpec(memory_space=pl.ANY)
        specs = [
            pl.BlockSpec(memory_space=pltpu.SMEM) if number < smem else whole(arg.shape)
            for number, arg in enumerate(args)
        ]
        for number in far:
            specs[number] = hbm
        out_specs = [
            hbm if number in far_out else whole(out.shape) for number, out in enumerate(outs)
        ]
        results = pl.pallas_call(
            kernel,
            grid=(1,),
            out_shape=outs,
            in_specs=specs,
            out_specs=out_specs,
            input_output_aliases=alias or {},
            scratch_shapes=list(scratch),
            compiler_params=pltpu.CompilerParams(vmem_limit_bytes=limit * 1024 * 1024),
            cost_estimate=pl.CostEstimate(
                flops=flops, bytes_accessed=4000000, transcendentals=0
            ),
        )(*args)
        return results[0] if single else results

    return run


def pack_kernel(x_ref, pos_ref, bias_ref, cot_ref, near_ref, pack_ref, face_ref):
    pack_ref[0:N, :] = x_ref[...]
    face_ref[0:N, :] = cot_ref[...]
    zeros = jnp.zeros((16, D - N), BF)
    small = jnp.concatenate(
        [pos_ref[...].astype(F32), bias_ref[...].astype(F32), jnp.zeros((5, N), F32)], axis=0
    )
    pack_ref[N : N + 16, :] = jnp.concatenate([small.astype(BF), zeros], axis=1)
    near = jnp.broadcast_to(near_ref[...].astype(F32), (16, N)).astype(BF)
    face_ref[N : N + 16, :] = jnp.concatenate([near, zeros], axis=1)


def split_kernel(place_ref, keep_ref, recv_ref, *outs):
    for step, out in enumerate(outs):
        chunk = lax.rem(place_ref[0] + step, 4)
        rows = pl.ds(chunk * 4, 4)
        total = keep_ref[rows].astype(F32) + recv_ref[rows].astype(F32)
        out[...] = total.astype(out.dtype)


def resplit_kernel(place_ref, own_ref, a_ref, b_ref, c_ref, *outs):
    for step, out in enumerate(outs):
        chunk = lax.rem(place_ref[1] + step, 4)
        total = own_ref[chunk] + a_ref[chunk].astype(F32)
        total = total + b_ref[chunk].astype(F32) + c_ref[chunk].astype(F32)
        out[...] = total.astype(out.dtype)


def join_kernel(own_ref, a_ref, b_ref, c_ref, out_ref):
    total = own_ref[...] + a_ref[...].astype(F32)
    out_ref[...] = (total + b_ref[...].astype(F32) + c_ref[...].astype(F32)).astype(BF)


def pair_kernel(a_ref, b_ref, out_ref):
    out_ref[...] = (a_ref[...].astype(F32) + b_ref[...].astype(F32)).astype(BF)


def finish_kernel(whose, place_ref, *refs):
    parts, refs = refs[:4], refs[4 + 5 * whose :]
    outs, stage, sems = refs[:5], refs[5], refs[6]
    core = place_ref[2]
    side = core if whose == 0 else 1 - core
    copies = []
    for number in range(5):
        rows = slice(number * 16, (number + 1) * 16)
        for big in range(4):
            outer = lax.rem(place_ref[whose] + 4 - big, 4)
            for little in range(4):
                inner = lax.rem(place_ref[1 - whose] + 4 - little, 4)
                start = pl.multiple_of(outer * 64 + inner * 16, 16)
                piece = parts[big][little, rows, :]
                stage[number, pl.ds(start, 16), :] = piece.astype(F32)
        target = outs[number].at[pl.ds(pl.multiple_of(side * 256, 256), 256), :]
        copy = pltpu.make_async_copy(stage.at[number], target, sems.at[number])
        copy.start()
        copies.append(copy)
    for copy in copies:
        copy.wait()


def out_kernel(near_ref, low_ref, high_ref, mixed_ref, wf_ref, out_ref):
    row = lax.broadcasted_iota(jnp.int32, (2 * N, N), 0)
    pick = jnp.where(row == near_ref[...], 1.0, 0.0).astype(BF)
    received = jnp.concatenate([low_ref[...], high_ref[...]], axis=0)
    picked = dot(pick, received, 0, 0).astype(BF)
    out_ref[...] = (mixed_ref[...].astype(F32) + dot(picked, wf_ref[...])).astype(BF)


def add_kernel(one_ref, two_ref, recv_ref, to_one_ref, to_two_ref):
    to_one_ref[...] = (one_ref[...] + recv_ref[1].astype(F32)).astype(BF)
    to_two_ref[...] = (two_ref[...] + recv_ref[2].astype(F32)).astype(BF)


def input_kernel(own_ref, recv_ref, a_ref, b_ref, far_ref, dmix_ref, x_ref, gain_ref, out_ref):
    total = own_ref[...] + recv_ref[0].astype(F32) + a_ref[...].astype(F32)
    total = total + b_ref[...].astype(F32) + far_ref[...].astype(F32)
    scaled = gain_ref[...] * total.T
    x = x_ref[...].astype(F32)
    inverse = lax.rsqrt(jnp.mean(x * x, axis=1, keepdims=True) + EPS)
    drop = x * (inverse * inverse * inverse) * jnp.mean(scaled * x, axis=1, keepdims=True)
    out_ref[...] = (dmix_ref[...] + inverse * scaled - drop).astype(BF)


def device_order(slabs, planes, move):
    rings = slabs // 4
    pairs = []
    for s in range(slabs):
        for p in range(planes):
            c, z, y_hi = s % 2, (s // 2) % rings, s // (2 * rings)
            x, y_lo = p // 2, p % 2
            z2, x2, y2 = move(c, z, x, 2 * y_hi + y_lo)
            y2 = y2 % 4
            s2 = ((y2 // 2) * rings + z2 % rings) * 2 + c
            pairs.append((s * planes + p, s2 * planes + (x2 % (planes // 2)) * 2 + y2 % 2))
    return pairs


def local(
    features,
    gain,
    w_query,
    w_key,
    w_value,
    w_out,
    w_face,
    gamma,
    positions,
    key_bias,
    block_mask,
    send_list,
    neighbour,
    cotangent,
):
    slabs, planes = lax.axis_size("slab"), lax.axis_size("plane")
    slab, plane = lax.axis_index("slab"), lax.axis_index("plane")
    core = slab % 2
    rings = slabs // 4
    x_at, y_at = plane // 2, (slab // (2 * rings)) * 2 + plane % 2

    def along(value, axis, target):
        return lax.ppermute(value, axis, [(i, target(i)) for i in range(lax.axis_size(axis))])

    def partner(value):
        return along(value, "slab", lambda s: s ^ 1)

    def near1(value):
        return along(value, "slab", lambda s: (s + 1 if s % 2 else s - 1) % slabs)

    def near2(value):
        return along(value, "slab", lambda s: (s - 2 if s % 2 else s + 2) % slabs)

    def near2_back(value):
        return along(value, "slab", lambda s: (s + 2 if s % 2 else s - 2) % slabs)

    def near3(value):
        return along(value, "slab", lambda s: (s + 3 if s % 2 else s - 3) % slabs)

    def opposite3(value):
        return along(value, "slab", lambda s: (s - 3 if s % 2 else s + 3) % slabs)

    def plane_step(value, steps):
        return along(value, "plane", lambda p: (p + steps) % planes)

    def outer_step(value, k):
        pairs = device_order(
            slabs, planes, lambda c, z, x, y: (z, x, y + k) if c else (z, x + k, y)
        )
        return lax.ppermute(value, BOTH, pairs)

    def inner_step(value, k):
        pairs = device_order(
            slabs, planes, lambda c, z, x, y: (z, x + k, y) if c else (z, x, y + k)
        )
        return lax.ppermute(value, BOTH, pairs)

    def z_flip(value, k):
        pairs = device_order(slabs, planes, lambda c, z, x, y: (z ^ k, x, y))
        return lax.ppermute(value, BOTH, pairs)

    tie = lax.optimization_barrier
    packed = shape((N + 16, D), BF)
    pack, face_pack = call(pack_kernel, (packed, packed), limit=60)(
        features, positions, key_bias, cotangent, neighbour[None]
    )
    got3 = near3(pack)
    fwd2 = opposite3(pack)
    got2 = near2(pack)
    fwd1 = near2_back(pack)
    got1 = near1(pack)
    fwd0 = partner(pack)
    got1, fwd0, face_pack = tie((got1, fwd0, face_pack))
    cot_dn = plane_step(face_pack, 1)
    cot_up = plane_step(face_pack, -1)

    offsets = (1 - 2 * core) * jnp.array([0, -1, -2, -3, 1, 2, 3], jnp.int32)
    allow = block_mask[0, 0][(slab + offsets) % slabs]
    half = core.astype(jnp.int32)[None]

    weight = pltpu.VMEM((D, D), BF)
    results = call(
        attend_kernel,
        (
            shape((16, 80, D), BF),
            shape((16, 80, D), BF),
            shape((N, D), BF),
            shape((N, D), BF),
            shape((N, D), BF),
            shape((N, D), F32),
            shape((D, N), F32),
            shape((3, D, N), BF),
            shape((D, N), F32),
            shape((D, N), F32),
            shape((D, N), BF),
        ),
        scratch=(
            *([weight] * 5),
            pltpu.SemaphoreType.DMA((5,)),
            pltpu.VMEM((16, 80, D), BF),
            pltpu.VMEM((16, 80, D), BF),
            pltpu.SemaphoreType.DMA((5,)),
            pltpu.SemaphoreType.DMA((5,)),
            pltpu.VMEM((D, KEYS), BF),
            pltpu.VMEM((D, KEYS), BF),
            pltpu.VMEM((D, KEYS), BF),
            pltpu.VMEM((N, D), BF),
            pltpu.VMEM((2, D, N), BF),
            pltpu.VMEM((KEYS, D), BF),
            pltpu.VMEM((KEYS, D), BF),
            pltpu.VMEM((KEYS, D), BF),
            pltpu.VMEM((KEYS, N), BF),
            pltpu.VMEM((HEADS * N, N), BF),
            pltpu.VMEM((N, D), BF),
        ),
        smem=4,
        flops=6000000000,
        limit=60,
        far=(16, 17, 18, 19, 20),
        far_out=(0, 1),
    )(
        offsets,
        allow,
        gamma,
        half,
        pack,
        got1,
        got2,
        got3,
        fwd0,
        fwd1,
        fwd2,
        cotangent,
        cot_dn,
        cot_up,
        send_list,
        gain[None],
        w_key,
        w_value,
        w_query,
        w_face,
        w_out,
    )
    send, keep, sent0, sent1, mixed, d_mixed = results[:6]
    dx_own, dx_part, dx_near1, dx_near2, dx_near3 = results[6:]
    got = partner(send)

    outer_at = jnp.where(core == 0, x_at, y_at)
    inner_at = jnp.where(core == 0, y_at, x_at)
    place = jnp.stack([outer_at, inner_at, core]).astype(jnp.int32)
    order = (2, 1, 3)
    chunk = shape((4, 80, D), BF)
    first = call(split_kernel, (shape((4, 80, D), F32), chunk, chunk, chunk), smem=1)(
        place, keep, got
    )
    first, dx_part, dx_near3 = tie((first, dx_part, dx_near3))
    got_first = [outer_step(first[k], k) for k in order]
    back = partner(dx_part)
    back3 = near3(dx_near3)
    got_first, back, back3 = tie((got_first, back, back3))

    chunk = shape((80, D), BF)
    second = call(resplit_kernel, (shape((80, D), F32), chunk, chunk, chunk), smem=1)(
        place, first[0], *got_first
    )
    got_second = [inner_step(second[k], k) for k in order]
    total = call(join_kernel, chunk)(second[0], *got_second)
    total = call(pair_kernel, chunk)(total, z_flip(total, 1))
    total = call(pair_kernel, chunk)(total, z_flip(total, 2))
    total, dx_near1, dx_near2 = tie((total, dx_near1, dx_near2))
    near = z_flip(total, 4)
    to_one, to_two = call(add_kernel, (shape((D, N), BF),) * 2)(dx_near1, dx_near2, back)
    near, to_one, to_two = tie((near, to_one, to_two))
    total = call(pair_kernel, chunk)(total, near)

    inner = {0: total}
    for k in order:
        inner[k] = inner_step(total, k)
    block = jnp.stack([inner[k] for k in range(4)])
    block, sent0, sent1, to_one, to_two = tie((block, sent0, sent1, to_one, to_two))
    outer = {0: block}
    for k in order:
        outer[k] = outer_step(block, k)
    back1 = near1(to_one)
    back2 = near2_back(to_two)
    face_low = plane_step(sent1, 1)
    face_high = plane_step(sent0, -1)
    mine = [outer[k] for k in range(4)]
    mine, face_low, face_high, back1, back2 = tie((mine, face_low, face_high, back1, back2))
    other = partner(mine)
    grads = (shape((D, D), F32),) * 5
    scratch = (pltpu.VMEM((5, 256, D), F32), pltpu.SemaphoreType.DMA((5,)))
    every = tuple(range(5))
    grads = call(
        functools.partial(finish_kernel, 0), grads, scratch, smem=1, far_out=every
    )(place, *mine)
    weights = call(
        functools.partial(finish_kernel, 1),
        (shape((D, D), F32),) * 5,
        scratch,
        smem=1,
        far=tuple(range(5, 10)),
        far_out=every,
        alias={5 + number: number for number in every},
    )(place, *other, *grads)
    d_out_w, d_face, d_query_w, d_key_w, d_value_w = weights

    out = call(out_kernel, shape((N, D), BF))(
        neighbour[None], face_low, face_high, mixed, w_face
    )
    d_input = call(input_kernel, shape((N, D), BF))(
        dx_own, back, back1, back2, back3, d_mixed, features, gain[None]
    )
    return (out, d_input, d_query_w, d_key_w, d_value_w, d_out_w, d_face)


def solution(mesh):
    rows = P(BOTH, None)
    return jax.shard_map(
        local,
        mesh=mesh,
        in_specs=(
            rows,
            P(),
            P(),
            P(),
            P(),
            P(),
            P(),
            P(),
            P(None, BOTH),
            P(None, BOTH),
            P("plane", "slab", None),
            P(None, BOTH),
            P(BOTH),
            rows,
        ),
        out_specs=(rows, rows, P(), P(), P(), P(), P()),
        check_vma=False,
    )
```

```python
import functools

import jax
import jax.numpy as jnp
from jax import lax
from jax.experimental import pallas as pl
from jax.experimental.pallas import tpu as pltpu
from jax.sharding import PartitionSpec as P

EPS = 1e-06
BF = jnp.bfloat16
F32 = jnp.float32
BOTH = ("slab", "plane")
N = 128
D = 512
HEADS = 8
WINDOW = 7
KEYS = WINDOW * N


def dot(a, b, ca=1, cb=0):
    return lax.dot_general(a, b, (((ca,), (cb,)), ((), ())), preferred_element_type=F32)


def pieces(value):
    high = value.astype(BF).astype(F32)
    rest = value - high
    mid = rest.astype(BF).astype(F32)
    return high, mid, rest - mid


def half_grads(stage, target, sems, start, normed_t, dk_t, dv_t, left, dq, d_mixed_b, grad_rows):
    copies = []
    rows = normed_t[pl.ds(start, 256), :]
    for number in range(5):
        if number == 0:
            grad = dot(left[0, pl.ds(start, 256), :], d_mixed_b)
        elif number == 1:
            grad = dot(left[1, pl.ds(start, 256), :], grad_rows)
        elif number == 2:
            grad = dot(rows[:, 0:N], dq)
        else:
            grad = dot(rows, (dk_t if number == 3 else dv_t)[...], 1, 1)
        grad = grad.astype(BF)
        part = slice(number * 16, (number + 1) * 16)
        for chunk in range(16):
            stage[chunk, part, :] = grad[chunk * 16 : (chunk + 1) * 16]
        copy = pltpu.make_async_copy(stage.at[:, part, :], target.at[:, part, :], sems.at[number])
        copy.start()
        copies.append(copy)
    return copies


def attend_kernel(
    offs_ref,
    allow_ref,
    gamma_ref,
    half_ref,
    own_ref,
    near1_ref,
    near2_ref,
    near3_ref,
    fwd0_ref,
    fwd1_ref,
    fwd2_ref,
    cot_ref,
    cot_dn_ref,
    cot_up_ref,
    list_ref,
    gain_ref,
    wk_hbm,
    wv_hbm,
    wq_hbm,
    wf_hbm,
    wo_hbm,
    send_ref,
    keep_ref,
    sent0_ref,
    sent1_ref,
    mixed_ref,
    dmix_ref,
    dx_own_ref,
    *refs,
):
    dx_part_ref, dx_near1_ref, dx_near2_ref, dx_near3_ref = refs[:4]
    refs = refs[4:]
    (
    wk_ref,
    wv_ref,
    wq_ref,
    wf_ref,
    wo_ref,
    weight_sems,
    send_stage,
    keep_stage,
    send_sems,
    keep_sems,
    normed_t_ref,
    dk_t_ref,
    dv_t_ref,
    dq_ref,
    left_ref,
    normed_ref,
    k_ref,
    v_ref,
    augk_ref,
    augq_ref,
    ho_ref,
    ) = refs
    loads = []
    for number, (source, target) in enumerate(
        (
            (wk_hbm, wk_ref),
            (wv_hbm, wv_ref),
            (wq_hbm, wq_ref),
            (wf_hbm, wf_ref),
            (wo_hbm, wo_ref),
        )
    ):
        load = pltpu.make_async_copy(source, target, weight_sems.at[number])
        load.start()
        loads.append(load)
    gain = gain_ref[...]
    blocks = (
        (own_ref, 0),
        (near1_ref, 0),
        (near2_ref, 0),
        (near3_ref, 0),
        (fwd0_ref, 0),
        (fwd1_ref, 0),
        (fwd2_ref, 0),
    )
    row16 = lax.broadcasted_iota(jnp.int32, (HEADS, 16, N), 1)
    axis = jnp.where(row16 < 12, row16 // 3, 4)
    gam = jnp.concatenate([jnp.full((1, 1), gamma_ref[h], F32) for h in range(HEADS)], axis=0)
    for number, (ref, start) in enumerate(blocks):
        rows = slice(number * N, (number + 1) * N)
        x = ref[start : start + N, :].astype(F32)
        inverse = lax.rsqrt(jnp.mean(x * x, axis=1, keepdims=True) + EPS)
        normed = (x * inverse * gain).astype(BF)
        normed_ref[rows, :] = normed
        normed_t_ref[:, rows] = normed.T
        small = ref[start + N : start + N + 16, 0:N].astype(F32)
        offset = offs_ref[number].astype(F32)
        px, py, pz = small[0:1], small[1:2], small[2:3]
        lifted = pz + offset
        norm2 = px * px + py * py + lifted * lifted
        bias = small[3:11] - gam * norm2
        bias = jnp.where(allow_ref[number] > 0, bias, -1e30)
        high, mid, low = pieces(bias)
        points = (px[None], py[None], pz[None])
        aug = jnp.where(axis == 3, offset, 0.0)
        for which, point in enumerate(points):
            aug = jnp.where(axis == which, point, aug)
        for which, piece in enumerate((high, mid, low)):
            aug = jnp.where(row16 == 12 + which, piece[:, None, :], aug)
        augk_ref[rows, :] = aug.reshape(N, N).T.astype(BF)
        if number == 0:
            aug = jnp.where(axis == 0, points[0], jnp.where(axis == 1, points[1], points[2]))
            high, mid, low = pieces(aug * (2.0 * gam[:, :, None]))
            aug = jnp.where(row16 % 3 == 0, high, jnp.where(row16 % 3 == 1, mid, low))
            aug = jnp.where(row16 < 12, aug, jnp.where(row16 < 15, 1.0, 0.0))
            augq_ref[...] = aug.reshape(N, N).T.astype(BF)

    for load in loads:
        load.wait()
    k_ref[...] = dot(normed_ref[...], wk_ref[...]).astype(BF)
    v_ref[...] = dot(normed_ref[...], wv_ref[...]).astype(BF)
    query = (dot(normed_ref[0:N, :], wq_ref[...]).astype(BF) * 0.125).astype(BF)

    row_n = lax.broadcasted_iota(jnp.int32, (N, N), 0)
    list0 = jnp.where(row_n == list_ref[0:1, :], 1.0, 0.0).astype(BF)
    list1 = jnp.where(row_n == list_ref[1:2, :], 1.0, 0.0).astype(BF)
    row_f = row_n.astype(F32)
    even = half_ref[1] == 0
    cot_one, cot_two = cot_up_ref[...], cot_dn_ref[...]
    cot_up = jnp.where(even, cot_one, cot_two)
    cot_dn = jnp.where(even, cot_two, cot_one)
    near_up = cot_up[N : N + 16, 0:N].astype(F32)[0:1]
    near_dn = cot_dn[N : N + 16, 0:N].astype(F32)[0:1]
    pick_up = jnp.where(row_f == near_up, 1.0, 0.0).astype(BF)
    pick_dn = jnp.where(row_f + 128.0 == near_dn, 1.0, 0.0).astype(BF)
    grad_rows = dot(dot(list1, pick_up).astype(BF), cot_up[0:N, :])
    grad_rows = grad_rows + dot(dot(list0, pick_dn).astype(BF), cot_dn[0:N, :])
    grad_rows = grad_rows.astype(BF)
    d_mixed = cot_ref[...].astype(F32) + dot(grad_rows, wf_ref[...], 1, 1)
    dmix_ref[...] = d_mixed
    d_mixed_b = d_mixed.astype(BF)
    d_heads = dot(d_mixed_b, wo_ref[...], 1, 1).astype(BF)

    lane = lax.broadcasted_iota(jnp.int32, (N, N), 1)
    first = lane < 64
    masks = (first, jnp.logical_not(first))
    masks_b = tuple(jnp.where(m, 1.0, 0.0).astype(BF) for m in masks)
    for pair in range(HEADS // 2):
        cols = slice(pair * N, (pair + 1) * N)
        keys = k_ref[:, cols]
        values = v_ref[:, cols]
        keys_aug = jnp.concatenate([keys, augk_ref[...]], axis=1)
        qp = query[:, cols]
        gp = d_heads[:, cols]
        q_parts = [qp * m for m in masks_b]
        g_parts = [gp * m for m in masks_b]
        probs = []
        probs_b = []
        outs = []
        for t in range(2):
            h = 2 * pair + t
            mine = jnp.where(lane // 16 == h, 1.0, 0.0).astype(BF)
            left = jnp.concatenate([q_parts[t], augq_ref[...] * mine], axis=1)
            scores = dot(left, keys_aug, 1, 1)
            top = jnp.max(scores, axis=1, keepdims=True)
            weights = jnp.exp(scores - top)
            prob = weights * (1.0 / jnp.sum(weights, axis=1, keepdims=True))
            probs.append(prob)
            probs_b.append(prob.astype(BF))
            outs.append(dot(probs_b[t], values))
        merged = jnp.where(first, outs[0], outs[1]).astype(BF)
        ho_ref[:, cols] = merged
        inner = gp.astype(F32) * merged.astype(F32)
        scores_b = []
        dqs = []
        for t in range(2):
            delta = jnp.sum(jnp.where(masks[t], inner, 0.0), axis=1, keepdims=True)
            d_prob = dot(g_parts[t], values, 1, 1)
            d_score = (probs[t] * (d_prob - delta)).astype(BF)
            scores_b.append(d_score)
            dqs.append(dot(d_score, keys))
        dq_ref[:, cols] = (jnp.where(first, dqs[0], dqs[1]) * 0.125).astype(BF)
        dk_t_ref[cols, :] = dot(
            jnp.concatenate(q_parts, axis=0), jnp.concatenate(scores_b, axis=0), 0, 0
        ).astype(BF)
        dv_t_ref[cols, :] = dot(
            jnp.concatenate(g_parts, axis=0), jnp.concatenate(probs_b, axis=0), 0, 0
        ).astype(BF)

    heads_out = ho_ref[...]
    mixed = (own_ref[0:N, :].astype(F32) + dot(heads_out, wo_ref[...])).astype(BF)
    mixed_ref[...] = mixed
    left_ref[0] = heads_out.T
    left_ref[1] = mixed.T
    mine = half_ref[0]
    dq = dq_ref[...]
    copies = []
    for stage, target, sems, side in (
        (send_stage, send_ref, send_sems, 1 - mine),
        (keep_stage, keep_ref, keep_sems, mine),
    ):
        copies += half_grads(
            stage,
            target,
            sems,
            pl.multiple_of(side * 256, 256),
            normed_t_ref,
            dk_t_ref,
            dv_t_ref,
            left_ref,
            dq,
            d_mixed_b,
            grad_rows,
        )

    dx_t = dot(wk_ref[...], dk_t_ref[...]) + dot(wv_ref[...], dv_t_ref[...])
    dx_own_ref[...] = dx_t[:, 0:N] + dot(wq_ref[...], dq, 1, 1)
    dx_near1_ref[...] = dx_t[:, N : 2 * N]
    dx_near2_ref[...] = dx_t[:, 2 * N : 3 * N]
    dx_near3_ref[...] = dx_t[:, 3 * N : 4 * N].astype(BF)
    for number in range(3):
        first = (4 + number) * N
        dx_part_ref[number] = dx_t[:, first : first + N].astype(BF)
    sent0_ref[...] = dot(jnp.where(even, list1, list0), mixed, 0, 0).astype(BF)
    sent1_ref[...] = dot(jnp.where(even, list0, list1), mixed, 0, 0).astype(BF)
    for copy in copies:
        copy.wait()


def shape(dims, kind):
    return jax.ShapeDtypeStruct(dims, kind)


def whole(dims):
    return pl.BlockSpec(dims, lambda i: (0,) * len(dims), pipeline_mode=pl.Buffered(1))


def call(kernel, outs, scratch=(), smem=0, flops=1000000, limit=16, far=(), far_out=(), alias=None):
    single = not isinstance(outs, tuple)
    outs = (outs,) if single else outs

    def run(*args):
        hbm = pl.BlockSpec(memory_space=pl.ANY)
        specs = [
            pl.BlockSpec(memory_space=pltpu.SMEM) if number < smem else whole(arg.shape)
            for number, arg in enumerate(args)
        ]
        for number in far:
            specs[number] = hbm
        out_specs = [
            hbm if number in far_out else whole(out.shape) for number, out in enumerate(outs)
        ]
        results = pl.pallas_call(
            kernel,
            grid=(1,),
            out_shape=outs,
            in_specs=specs,
            out_specs=out_specs,
            input_output_aliases=alias or {},
            scratch_shapes=list(scratch),
            compiler_params=pltpu.CompilerParams(vmem_limit_bytes=limit * 1024 * 1024),
            cost_estimate=pl.CostEstimate(
                flops=flops, bytes_accessed=4000000, transcendentals=0
            ),
        )(*args)
        return results[0] if single else results

    return run


def pack_kernel(x_ref, pos_ref, bias_ref, cot_ref, near_ref, pack_ref, face_ref):
    pack_ref[0:N, :] = x_ref[...]
    face_ref[0:N, :] = cot_ref[...]
    zeros = jnp.zeros((16, D - N), BF)
    small = jnp.concatenate(
        [pos_ref[...].astype(F32), bias_ref[...].astype(F32), jnp.zeros((5, N), F32)], axis=0
    )
    pack_ref[N : N + 16, :] = jnp.concatenate([small.astype(BF), zeros], axis=1)
    near = jnp.broadcast_to(near_ref[...].astype(F32), (16, N)).astype(BF)
    face_ref[N : N + 16, :] = jnp.concatenate([near, zeros], axis=1)


def hold_kernel(keep_ref, out_ref, sem):
    copy = pltpu.make_async_copy(keep_ref, out_ref, sem)
    copy.start()
    copy.wait()


def hold(value):
    return pl.pallas_call(
        hold_kernel,
        out_shape=shape(value.shape, value.dtype),
        in_specs=[pl.BlockSpec(memory_space=pl.ANY)],
        out_specs=pl.BlockSpec(memory_space=pltpu.VMEM),
        scratch_shapes=[pltpu.SemaphoreType.DMA],
        compiler_params=pltpu.CompilerParams(vmem_limit_bytes=8 * 1024 * 1024),
        cost_estimate=pl.CostEstimate(
            flops=1000000000, bytes_accessed=4000000, transcendentals=0
        ),
    )(value)


def split_kernel(place_ref, keep_ref, recv_ref, *outs):
    for step, out in enumerate(outs):
        rows = pl.ds((place_ref[0] ^ step) * 4, 4)
        total = keep_ref[rows].astype(F32) + recv_ref[rows].astype(F32)
        out[...] = total.astype(out.dtype)


def resplit_kernel(place_ref, own_ref, a_ref, b_ref, c_ref, *outs):
    for step, out in enumerate(outs):
        chunk = place_ref[1] ^ step
        total = own_ref[chunk] + a_ref[chunk].astype(F32)
        total = total + b_ref[chunk].astype(F32) + c_ref[chunk].astype(F32)
        out[...] = total.astype(out.dtype)


def join_kernel(own_ref, a_ref, b_ref, c_ref, out_ref):
    total = own_ref[...] + a_ref[...].astype(F32)
    out_ref[...] = (total + b_ref[...].astype(F32) + c_ref[...].astype(F32)).astype(BF)


def pair_kernel(a_ref, b_ref, out_ref):
    out_ref[...] = (a_ref[...].astype(F32) + b_ref[...].astype(F32)).astype(BF)


def finish_kernel(whose, place_ref, *refs):
    parts, refs = refs[:4], refs[5 + 4 * whose :]
    outs, stage, sems = refs[:5], refs[5], refs[6]
    core = place_ref[2]
    side = core if whose == 0 else 1 - core
    copies = []
    for number in range(5):
        rows = slice(number * 16, (number + 1) * 16)
        for big in range(4):
            outer = place_ref[whose] ^ big
            for little in range(4):
                inner = place_ref[1 - whose] ^ little
                start = pl.multiple_of(outer * 64 + inner * 16, 16)
                piece = parts[big][little, rows, :]
                stage[number, pl.ds(start, 16), :] = piece.astype(F32)
        target = outs[number].at[pl.ds(pl.multiple_of(side * 256, 256), 256), :]
        copy = pltpu.make_async_copy(stage.at[number], target, sems.at[number])
        copy.start()
        copies.append(copy)
    for copy in copies:
        copy.wait()


def out_kernel(parity_ref, near_ref, one_ref, two_ref, mixed_ref, wf_ref, out_ref):
    even = parity_ref[1] == 0
    one, two = one_ref[...], two_ref[...]
    row = lax.broadcasted_iota(jnp.int32, (2 * N, N), 0)
    pick = jnp.where(row == near_ref[...], 1.0, 0.0).astype(BF)
    received = jnp.concatenate([jnp.where(even, two, one), jnp.where(even, one, two)], axis=0)
    picked = dot(pick, received, 0, 0).astype(BF)
    out_ref[...] = (mixed_ref[...].astype(F32) + dot(picked, wf_ref[...])).astype(BF)


def add_kernel(one_ref, two_ref, recv_ref, to_one_ref, to_two_ref):
    to_one_ref[...] = (one_ref[...] + recv_ref[1].astype(F32)).astype(BF)
    to_two_ref[...] = (two_ref[...] + recv_ref[2].astype(F32)).astype(BF)


def input_kernel(own_ref, *refs):
    parts, (dmix_ref, x_ref, gain_ref, out_ref) = refs[:4], refs[4:]
    total = own_ref[...]
    for part in parts:
        total = total + (part[0] if len(part.shape) == 3 else part[...]).astype(F32)
    scaled = gain_ref[...] * total.T
    x = x_ref[...].astype(F32)
    inverse = lax.rsqrt(jnp.mean(x * x, axis=1, keepdims=True) + EPS)
    drop = x * (inverse * inverse * inverse) * jnp.mean(scaled * x, axis=1, keepdims=True)
    out_ref[...] = (dmix_ref[...] + inverse * scaled - drop).astype(BF)


def device_order(slabs, planes, move):
    rings = slabs // 4
    pairs = []
    for s in range(slabs):
        for p in range(planes):
            c, z, y_hi = s % 2, (s // 2) % rings, s // (2 * rings)
            x, y_lo = p // 2, p % 2
            z2, x2, y2 = move(c, z, x, 2 * y_hi + y_lo)
            y2 = y2 % 4
            s2 = ((y2 // 2) * rings + z2 % rings) * 2 + c
            pairs.append((s * planes + p, s2 * planes + (x2 % (planes // 2)) * 2 + y2 % 2))
    return pairs


def local(
    features,
    gain,
    w_query,
    w_key,
    w_value,
    w_out,
    w_face,
    gamma,
    positions,
    key_bias,
    block_mask,
    send_list,
    neighbour,
    cotangent,
):
    slabs, planes = lax.axis_size("slab"), lax.axis_size("plane")
    slab, plane = lax.axis_index("slab"), lax.axis_index("plane")
    core = slab % 2
    rings = slabs // 4
    x_at, y_at = plane // 2, (slab // (2 * rings)) * 2 + plane % 2

    def along(value, axis, target):
        return lax.ppermute(value, axis, [(i, target(i)) for i in range(lax.axis_size(axis))])

    def partner(value):
        return along(value, "slab", lambda s: s ^ 1)

    def near1(value):
        return along(value, "slab", lambda s: (s + 1 if s % 2 else s - 1) % slabs)

    def near2(value):
        return along(value, "slab", lambda s: (s - 2 if s % 2 else s + 2) % slabs)

    def near2_back(value):
        return along(value, "slab", lambda s: (s + 2 if s % 2 else s - 2) % slabs)

    def near3(value):
        return along(value, "slab", lambda s: (s + 3 if s % 2 else s - 3) % slabs)

    def opposite3(value):
        return along(value, "slab", lambda s: (s - 3 if s % 2 else s + 3) % slabs)

    def plane_pair(value):
        return along(value, "plane", lambda p: p ^ 1)

    def plane_cross(value):
        return along(value, "plane", lambda p: (p + 1 if p % 2 else p - 1) % planes)

    def outer_step(value, k):
        pairs = device_order(
            slabs, planes, lambda c, z, x, y: (z, x, y ^ k) if c else (z, x ^ k, y)
        )
        return lax.ppermute(value, BOTH, pairs)

    def inner_step(value, k):
        pairs = device_order(
            slabs, planes, lambda c, z, x, y: (z, x ^ k, y) if c else (z, x, y ^ k)
        )
        return lax.ppermute(value, BOTH, pairs)

    def z_flip(value, k):
        pairs = device_order(slabs, planes, lambda c, z, x, y: (z ^ k, x, y))
        return lax.ppermute(value, BOTH, pairs)

    tie = lax.optimization_barrier
    packed = shape((N + 16, D), BF)
    pack, face_pack = call(pack_kernel, (packed, packed), limit=60)(
        features, positions, key_bias, cotangent, neighbour[None]
    )
    cot_one = plane_pair(face_pack)
    cot_two = plane_cross(face_pack)
    fwd2 = opposite3(pack)
    got3 = near3(pack)
    got2 = near2(pack)
    fwd1 = near2_back(pack)
    cot_one, cot_two, near_pack = tie((cot_one, cot_two, pack))
    got1 = near1(near_pack)
    fwd0 = partner(near_pack)

    offsets = (1 - 2 * core) * jnp.array([0, -1, -2, -3, 1, 2, 3], jnp.int32)
    allow = block_mask[0, 0][(slab + offsets) % slabs]
    half = jnp.stack([core, plane % 2]).astype(jnp.int32)

    weight = pltpu.VMEM((D, D), BF)
    results = call(
        attend_kernel,
        (
            shape((16, 80, D), BF),
            shape((16, 80, D), BF),
            shape((N, D), BF),
            shape((N, D), BF),
            shape((N, D), BF),
            shape((N, D), F32),
            shape((D, N), F32),
            shape((3, D, N), BF),
            shape((D, N), F32),
            shape((D, N), F32),
            shape((D, N), BF),
        ),
        scratch=(
            *([weight] * 5),
            pltpu.SemaphoreType.DMA((5,)),
            pltpu.VMEM((16, 80, D), BF),
            pltpu.VMEM((16, 80, D), BF),
            pltpu.SemaphoreType.DMA((5,)),
            pltpu.SemaphoreType.DMA((5,)),
            pltpu.VMEM((D, KEYS), BF),
            pltpu.VMEM((D, KEYS), BF),
            pltpu.VMEM((D, KEYS), BF),
            pltpu.VMEM((N, D), BF),
            pltpu.VMEM((2, D, N), BF),
            pltpu.VMEM((KEYS, D), BF),
            pltpu.VMEM((KEYS, D), BF),
            pltpu.VMEM((KEYS, D), BF),
            pltpu.VMEM((KEYS, N), BF),
            pltpu.VMEM((N, N), BF),
            pltpu.VMEM((N, D), BF),
        ),
        smem=4,
        flops=6000000000,
        limit=60,
        far=(16, 17, 18, 19, 20),
        far_out=(0, 1),
    )(
        offsets,
        allow,
        gamma,
        half,
        pack,
        got1,
        got2,
        got3,
        fwd0,
        fwd1,
        fwd2,
        cotangent,
        cot_two,
        cot_one,
        send_list,
        gain[None],
        w_key,
        w_value,
        w_query,
        w_face,
        w_out,
    )
    send, keep, sent0, sent1, mixed, d_mixed = results[:6]
    dx_own, dx_part, dx_near1, dx_near2, dx_near3 = results[6:]
    got = partner(send)
    keep = hold(keep)

    outer_at = jnp.where(core == 0, x_at, y_at)
    inner_at = jnp.where(core == 0, y_at, x_at)
    place = jnp.stack([outer_at, inner_at, core]).astype(jnp.int32)
    order = (2, 1, 3)
    chunk = shape((4, 80, D), BF)
    first = call(split_kernel, (shape((4, 80, D), F32), chunk, chunk, chunk), smem=1)(
        place, keep, got
    )
    first, dx_part, dx_near3 = tie((first, dx_part, dx_near3))
    got_first = [outer_step(first[k], k) for k in order]
    back = partner(dx_part)
    back3 = near3(dx_near3)
    got_first, back, back3 = tie((got_first, back, back3))

    chunk = shape((80, D), BF)
    second = call(resplit_kernel, (shape((80, D), F32), chunk, chunk, chunk), smem=1)(
        place, first[0], *got_first
    )
    second, sent0, sent1 = tie((second, sent0, sent1))
    got_second = [inner_step(second[k], k) for k in order]
    face_one = plane_pair(sent0)
    face_two = plane_cross(sent1)
    got_second, face_one, face_two = tie((got_second, face_one, face_two))
    total = call(join_kernel, chunk)(second[0], *got_second)
    total = call(pair_kernel, chunk)(total, z_flip(total, 1))
    total, face_one, face_two = tie((total, face_one, face_two))
    near = z_flip(total, 2)
    out = call(out_kernel, shape((N, D), BF), smem=1)(
        half, neighbour[None], face_one, face_two, mixed, w_face
    )
    near, out = tie((near, out))
    total = call(pair_kernel, chunk)(total, near)
    total, dx_near1, dx_near2 = tie((total, dx_near1, dx_near2))
    near = z_flip(total, 4)
    to_one, to_two = call(add_kernel, (shape((D, N), BF),) * 2)(dx_near1, dx_near2, back)
    near, to_one, to_two = tie((near, to_one, to_two))
    total = call(pair_kernel, chunk)(total, near)

    total, meet = tie((total, partner(total)))
    inner = {0: total}
    for k in order:
        inner[k] = inner_step(total, k)
    block = jnp.stack([inner[k] for k in range(4)])
    block, to_one, to_two = tie((block, to_one, to_two))
    outer = {0: block}
    for k in order:
        outer[k] = outer_step(block, k)
    back1 = near1(to_one)
    back2 = near2_back(to_two)
    mine = [outer[k] for k in range(4)]
    mine, back1, back2 = tie((mine, back1, back2))
    other = partner(mine)
    grads = (shape((D, D), F32),) * 5
    scratch = (pltpu.VMEM((5, 256, D), F32), pltpu.SemaphoreType.DMA((5,)))
    every = tuple(range(5))
    grads = call(
        functools.partial(finish_kernel, 0), grads, scratch, smem=1, far=(5,), far_out=every
    )(place, *mine, meet)
    weights = call(
        functools.partial(finish_kernel, 1),
        (shape((D, D), F32),) * 5,
        scratch,
        smem=1,
        far=tuple(range(5, 10)),
        far_out=every,
        alias={5 + number: number for number in every},
    )(place, *other, *grads)
    d_out_w, d_face, d_query_w, d_key_w, d_value_w = weights

    d_input = call(input_kernel, shape((N, D), BF))(
        dx_own, back, back1, back2, back3, d_mixed, features, gain[None]
    )
    return (out, d_input, d_query_w, d_key_w, d_value_w, d_out_w, d_face)


def solution(mesh):
    rows = P(BOTH, None)
    return jax.shard_map(
        local,
        mesh=mesh,
        in_specs=(
            rows,
            P(),
            P(),
            P(),
            P(),
            P(),
            P(),
            P(),
            P(None, BOTH),
            P(None, BOTH),
            P("plane", "slab", None),
            P(None, BOTH),
            P(BOTH),
            rows,
        ),
        out_specs=(rows, rows, P(), P(), P(), P(), P()),
        check_vma=False,
    )
```

```python
import functools

import jax
import jax.numpy as jnp
from jax import lax
from jax.experimental import pallas as pl
from jax.experimental.pallas import tpu as pltpu
from jax.sharding import PartitionSpec as P

EPS = 1e-06
BF = jnp.bfloat16
F32 = jnp.float32
BOTH = ("slab", "plane")
N = 128
D = 512
HEADS = 8
WINDOW = 7
KEYS = WINDOW * N


def dot(a, b, ca=1, cb=0):
    return lax.dot_general(a, b, (((ca,), (cb,)), ((), ())), preferred_element_type=F32)


def pieces(value):
    high = value.astype(BF).astype(F32)
    rest = value - high
    mid = rest.astype(BF).astype(F32)
    return high, mid, rest - mid


def half_grads(stage, target, sems, start, normed_t, dk_t, dv_t, left, dq, d_mixed_b, grad_rows):
    copies = []
    rows = normed_t[pl.ds(start, 256), :]
    for number in range(5):
        if number == 0:
            grad = dot(left[0, pl.ds(start, 256), :], d_mixed_b)
        elif number == 1:
            grad = dot(left[1, pl.ds(start, 256), :], grad_rows)
        elif number == 2:
            grad = dot(rows[:, 0:N], dq)
        else:
            grad = dot(rows, (dk_t if number == 3 else dv_t)[...], 1, 1)
        grad = grad.astype(BF)
        part = slice(number * 16, (number + 1) * 16)
        for chunk in range(16):
            stage[chunk, part, :] = grad[chunk * 16 : (chunk + 1) * 16]
        copy = pltpu.make_async_copy(stage.at[:, part, :], target.at[:, part, :], sems.at[number])
        copy.start()
        copies.append(copy)
    return copies


def attend_kernel(offs_ref, allow_ref, gamma_ref, half_ref, *refs):
    pack_hbm, refs = refs[:7], refs[7:]
    cot_hbm, refs = refs[:3], refs[3:]
    list_ref, gain_ref, refs = refs[0], refs[1], refs[2:]
    weight_hbm, refs = refs[:5], refs[5:]
    send_ref, keep_ref, refs = refs[0], refs[1], refs[2:]
    out_hbm, refs = refs[:9], refs[9:]
    wk_ref, wv_ref, wq_ref, wf_ref, wo_ref = weight_refs = refs[:5]
    weight_sems, send_stage, keep_stage, send_sems, keep_sems = refs[5:10]
    normed_t_ref, dk_t_ref, dv_t_ref, dq_ref, left_ref = refs[10:15]
    normed_ref, k_ref, v_ref, augk_ref, augq_ref, ho_ref = refs[15:21]
    packs, cot_pair, cot_ref, in_sems, out_sems = refs[21:26]
    stages = refs[26:]
    sent0_ref, sent1_ref, mixed_ref, dmix_ref, dx_own_ref = stages[:5]
    dx_part_ref, dx_near1_ref, dx_near2_ref, dx_near3_ref = stages[5:]

    arrivals = []
    for number, source in enumerate(pack_hbm):
        copy = pltpu.make_async_copy(source, packs.at[number], in_sems.at[number])
        copy.start()
        arrivals.append(copy)
    loads = []
    for number, (source, target) in enumerate(zip(weight_hbm, weight_refs)):
        load = pltpu.make_async_copy(source, target, weight_sems.at[number])
        load.start()
        loads.append(load)
    cot_targets = (cot_ref, cot_pair.at[0], cot_pair.at[1])
    for number, (source, target) in enumerate(zip(cot_hbm, cot_targets)):
        load = pltpu.make_async_copy(source, target, in_sems.at[7 + number])
        load.start()
        loads.append(load)
    copies = []

    def flush(*numbers):
        for number in numbers:
            copy = pltpu.make_async_copy(stages[number], out_hbm[number], out_sems.at[number])
            copy.start()
            copies.append(copy)

    gain = gain_ref[...]
    row16 = lax.broadcasted_iota(jnp.int32, (HEADS, 16, N), 1)
    axis = jnp.where(row16 < 12, row16 // 3, 4)
    gam = jnp.concatenate([jnp.full((1, 1), gamma_ref[h], F32) for h in range(HEADS)], axis=0)
    for number in range(7):
        arrivals[number].wait()
        rows = slice(number * N, (number + 1) * N)
        x = packs[number, 0:N, :].astype(F32)
        inverse = lax.rsqrt(jnp.mean(x * x, axis=1, keepdims=True) + EPS)
        normed = (x * inverse * gain).astype(BF)
        normed_ref[rows, :] = normed
        normed_t_ref[:, rows] = normed.T
        small = packs[number, N : N + 16, 0:N].astype(F32)
        offset = offs_ref[number].astype(F32)
        px, py, pz = small[0:1], small[1:2], small[2:3]
        lifted = pz + offset
        norm2 = px * px + py * py + lifted * lifted
        bias = small[3:11] - gam * norm2
        bias = jnp.where(allow_ref[number] > 0, bias, -1e30)
        high, mid, low = pieces(bias)
        points = (px[None], py[None], pz[None])
        aug = jnp.where(axis == 3, offset, 0.0)
        for which, point in enumerate(points):
            aug = jnp.where(axis == which, point, aug)
        for which, piece in enumerate((high, mid, low)):
            aug = jnp.where(row16 == 12 + which, piece[:, None, :], aug)
        augk_ref[rows, :] = aug.reshape(N, N).T.astype(BF)
        if number == 0:
            aug = jnp.where(axis == 0, points[0], jnp.where(axis == 1, points[1], points[2]))
            high, mid, low = pieces(aug * (2.0 * gam[:, :, None]))
            aug = jnp.where(row16 % 3 == 0, high, jnp.where(row16 % 3 == 1, mid, low))
            aug = jnp.where(row16 < 12, aug, jnp.where(row16 < 15, 1.0, 0.0))
            augq_ref[...] = aug.reshape(N, N).T.astype(BF)

    for load in loads:
        load.wait()
    k_ref[...] = dot(normed_ref[...], wk_ref[...]).astype(BF)
    v_ref[...] = dot(normed_ref[...], wv_ref[...]).astype(BF)
    query = (dot(normed_ref[0:N, :], wq_ref[...]).astype(BF) * 0.125).astype(BF)

    row_n = lax.broadcasted_iota(jnp.int32, (N, N), 0)
    list0 = jnp.where(row_n == list_ref[0:1, :], 1.0, 0.0).astype(BF)
    list1 = jnp.where(row_n == list_ref[1:2, :], 1.0, 0.0).astype(BF)
    row_f = row_n.astype(F32)
    even = half_ref[1] == 0
    cot_two, cot_one = cot_pair[0], cot_pair[1]
    cot_up = jnp.where(even, cot_one, cot_two)
    cot_dn = jnp.where(even, cot_two, cot_one)
    near_up = cot_up[N : N + 16, 0:N].astype(F32)[0:1]
    near_dn = cot_dn[N : N + 16, 0:N].astype(F32)[0:1]
    pick_up = jnp.where(row_f == near_up, 1.0, 0.0).astype(BF)
    pick_dn = jnp.where(row_f + 128.0 == near_dn, 1.0, 0.0).astype(BF)
    grad_rows = dot(dot(list1, pick_up).astype(BF), cot_up[0:N, :])
    grad_rows = grad_rows + dot(dot(list0, pick_dn).astype(BF), cot_dn[0:N, :])
    grad_rows = grad_rows.astype(BF)
    d_mixed = cot_ref[...].astype(F32) + dot(grad_rows, wf_ref[...], 1, 1)
    dmix_ref[...] = d_mixed
    flush(3)
    d_mixed_b = d_mixed.astype(BF)
    d_heads = dot(d_mixed_b, wo_ref[...], 1, 1).astype(BF)

    lane = lax.broadcasted_iota(jnp.int32, (N, N), 1)
    first = lane < 64
    masks = (first, jnp.logical_not(first))
    masks_b = tuple(jnp.where(m, 1.0, 0.0).astype(BF) for m in masks)
    for pair in range(HEADS // 2):
        cols = slice(pair * N, (pair + 1) * N)
        keys = k_ref[:, cols]
        values = v_ref[:, cols]
        keys_aug = jnp.concatenate([keys, augk_ref[...]], axis=1)
        qp = query[:, cols]
        gp = d_heads[:, cols]
        q_parts = [qp * m for m in masks_b]
        g_parts = [gp * m for m in masks_b]
        probs = []
        probs_b = []
        outs = []
        for t in range(2):
            h = 2 * pair + t
            mine = jnp.where(lane // 16 == h, 1.0, 0.0).astype(BF)
            left = jnp.concatenate([q_parts[t], augq_ref[...] * mine], axis=1)
            scores = dot(left, keys_aug, 1, 1)
            top = jnp.max(scores, axis=1, keepdims=True)
            weights = jnp.exp(scores - top)
            prob = weights * (1.0 / jnp.sum(weights, axis=1, keepdims=True))
            probs.append(prob)
            probs_b.append(prob.astype(BF))
            outs.append(dot(probs_b[t], values))
        merged = jnp.where(first, outs[0], outs[1]).astype(BF)
        ho_ref[:, cols] = merged
        inner = gp.astype(F32) * merged.astype(F32)
        scores_b = []
        dqs = []
        for t in range(2):
            delta = jnp.sum(jnp.where(masks[t], inner, 0.0), axis=1, keepdims=True)
            d_prob = dot(g_parts[t], values, 1, 1)
            d_score = (probs[t] * (d_prob - delta)).astype(BF)
            scores_b.append(d_score)
            dqs.append(dot(d_score, keys))
        dq_ref[:, cols] = (jnp.where(first, dqs[0], dqs[1]) * 0.125).astype(BF)
        dk_t_ref[cols, :] = dot(
            jnp.concatenate(q_parts, axis=0), jnp.concatenate(scores_b, axis=0), 0, 0
        ).astype(BF)
        dv_t_ref[cols, :] = dot(
            jnp.concatenate(g_parts, axis=0), jnp.concatenate(probs_b, axis=0), 0, 0
        ).astype(BF)

    heads_out = ho_ref[...]
    mixed = (packs[0, 0:N, :].astype(F32) + dot(heads_out, wo_ref[...])).astype(BF)
    mixed_ref[...] = mixed
    sent0_ref[...] = dot(jnp.where(even, list1, list0), mixed, 0, 0).astype(BF)
    sent1_ref[...] = dot(jnp.where(even, list0, list1), mixed, 0, 0).astype(BF)
    flush(0, 1, 2)
    dq = dq_ref[...]
    dx_t = dot(wk_ref[...], dk_t_ref[...]) + dot(wv_ref[...], dv_t_ref[...])
    dx_own_ref[...] = dx_t[:, 0:N] + dot(wq_ref[...], dq, 1, 1)
    dx_near1_ref[...] = dx_t[:, N : 2 * N]
    dx_near2_ref[...] = dx_t[:, 2 * N : 3 * N]
    dx_near3_ref[...] = dx_t[:, 3 * N : 4 * N].astype(BF)
    for number in range(3):
        first = (4 + number) * N
        dx_part_ref[number] = dx_t[:, first : first + N].astype(BF)
    flush(4, 5, 6, 7, 8)

    left_ref[0] = heads_out.T
    left_ref[1] = mixed.T
    mine = half_ref[0]
    for stage, target, sems, side in (
        (send_stage, send_ref, send_sems, 1 - mine),
        (keep_stage, keep_ref, keep_sems, mine),
    ):
        copies += half_grads(
            stage,
            target,
            sems,
            pl.multiple_of(side * 256, 256),
            normed_t_ref,
            dk_t_ref,
            dv_t_ref,
            left_ref,
            dq,
            d_mixed_b,
            grad_rows,
        )

    for copy in copies:
        copy.wait()


def shape(dims, kind):
    return jax.ShapeDtypeStruct(dims, kind)


def whole(dims):
    return pl.BlockSpec(dims, lambda i: (0,) * len(dims), pipeline_mode=pl.Buffered(1))


def call(kernel, outs, scratch=(), smem=0, flops=1000000, limit=16, far=(), far_out=(), alias=None):
    single = not isinstance(outs, tuple)
    outs = (outs,) if single else outs

    def run(*args):
        hbm = pl.BlockSpec(memory_space=pl.ANY)
        specs = [
            pl.BlockSpec(memory_space=pltpu.SMEM) if number < smem else whole(arg.shape)
            for number, arg in enumerate(args)
        ]
        for number in far:
            specs[number] = hbm
        out_specs = [
            hbm if number in far_out else whole(out.shape) for number, out in enumerate(outs)
        ]
        results = pl.pallas_call(
            kernel,
            grid=(1,),
            out_shape=outs,
            in_specs=specs,
            out_specs=out_specs,
            input_output_aliases=alias or {},
            scratch_shapes=list(scratch),
            compiler_params=pltpu.CompilerParams(vmem_limit_bytes=limit * 1024 * 1024),
            cost_estimate=pl.CostEstimate(
                flops=flops, bytes_accessed=4000000, transcendentals=0
            ),
        )(*args)
        return results[0] if single else results

    return run


def pack_kernel(x_ref, pos_ref, bias_ref, cot_ref, near_ref, pack_ref, face_ref):
    pack_ref[0:N, :] = x_ref[...]
    face_ref[0:N, :] = cot_ref[...]
    zeros = jnp.zeros((16, D - N), BF)
    small = jnp.concatenate(
        [pos_ref[...].astype(F32), bias_ref[...].astype(F32), jnp.zeros((5, N), F32)], axis=0
    )
    pack_ref[N : N + 16, :] = jnp.concatenate([small.astype(BF), zeros], axis=1)
    near = jnp.broadcast_to(near_ref[...].astype(F32), (16, N)).astype(BF)
    face_ref[N : N + 16, :] = jnp.concatenate([near, zeros], axis=1)


def hold_kernel(keep_ref, out_ref, sem):
    copy = pltpu.make_async_copy(keep_ref, out_ref, sem)
    copy.start()
    copy.wait()


def hold(value):
    return pl.pallas_call(
        hold_kernel,
        out_shape=shape(value.shape, value.dtype),
        in_specs=[pl.BlockSpec(memory_space=pl.ANY)],
        out_specs=pl.BlockSpec(memory_space=pltpu.VMEM),
        scratch_shapes=[pltpu.SemaphoreType.DMA],
        compiler_params=pltpu.CompilerParams(vmem_limit_bytes=8 * 1024 * 1024),
        cost_estimate=pl.CostEstimate(
            flops=1000000000, bytes_accessed=4000000, transcendentals=0
        ),
    )(value)


def split_kernel(place_ref, keep_ref, recv_ref, *outs):
    for step, out in enumerate(outs):
        rows = pl.ds((place_ref[0] ^ step) * 4, 4)
        total = keep_ref[rows].astype(F32) + recv_ref[rows].astype(F32)
        out[...] = total.astype(out.dtype)


def resplit_kernel(place_ref, own_ref, a_ref, b_ref, c_ref, *outs):
    for step, out in enumerate(outs):
        chunk = place_ref[1] ^ step
        total = own_ref[chunk] + a_ref[chunk].astype(F32)
        total = total + b_ref[chunk].astype(F32) + c_ref[chunk].astype(F32)
        out[...] = total.astype(out.dtype)


def join_kernel(own_ref, a_ref, b_ref, c_ref, out_ref):
    total = own_ref[...] + a_ref[...].astype(F32)
    out_ref[...] = (total + b_ref[...].astype(F32) + c_ref[...].astype(F32)).astype(BF)


def pair_kernel(a_ref, b_ref, out_ref):
    out_ref[...] = (a_ref[...].astype(F32) + b_ref[...].astype(F32)).astype(BF)


def finish_kernel(whose, place_ref, *refs):
    parts, refs = refs[:4], refs[5 + 4 * whose :]
    outs, stage, sems = refs[:5], refs[5], refs[6]
    core = place_ref[2]
    side = core if whose == 0 else 1 - core
    copies = []
    for number in range(5):
        rows = slice(number * 16, (number + 1) * 16)
        for big in range(4):
            outer = place_ref[whose] ^ big
            for little in range(4):
                inner = place_ref[1 - whose] ^ little
                start = pl.multiple_of(outer * 64 + inner * 16, 16)
                piece = parts[big][little, rows, :]
                stage[number, pl.ds(start, 16), :] = piece.astype(F32)
        target = outs[number].at[pl.ds(pl.multiple_of(side * 256, 256), 256), :]
        copy = pltpu.make_async_copy(stage.at[number], target, sems.at[number])
        copy.start()
        copies.append(copy)
    for copy in copies:
        copy.wait()


def out_kernel(parity_ref, near_ref, one_ref, two_ref, mixed_ref, wf_ref, out_ref):
    even = parity_ref[1] == 0
    one, two = one_ref[...], two_ref[...]
    row = lax.broadcasted_iota(jnp.int32, (2 * N, N), 0)
    pick = jnp.where(row == near_ref[...], 1.0, 0.0).astype(BF)
    received = jnp.concatenate([jnp.where(even, two, one), jnp.where(even, one, two)], axis=0)
    picked = dot(pick, received, 0, 0).astype(BF)
    out_ref[...] = (mixed_ref[...].astype(F32) + dot(picked, wf_ref[...])).astype(BF)


def add_kernel(one_ref, two_ref, recv_ref, to_one_ref, to_two_ref):
    to_one_ref[...] = (one_ref[...] + recv_ref[1].astype(F32)).astype(BF)
    to_two_ref[...] = (two_ref[...] + recv_ref[2].astype(F32)).astype(BF)


def input_kernel(own_ref, *refs):
    parts, (dmix_ref, x_ref, gain_ref, out_ref) = refs[:4], refs[4:]
    total = own_ref[...]
    for part in parts:
        total = total + (part[0] if len(part.shape) == 3 else part[...]).astype(F32)
    scaled = gain_ref[...] * total.T
    x = x_ref[...].astype(F32)
    inverse = lax.rsqrt(jnp.mean(x * x, axis=1, keepdims=True) + EPS)
    drop = x * (inverse * inverse * inverse) * jnp.mean(scaled * x, axis=1, keepdims=True)
    out_ref[...] = (dmix_ref[...] + inverse * scaled - drop).astype(BF)


def device_order(slabs, planes, move):
    rings = slabs // 4
    pairs = []
    for s in range(slabs):
        for p in range(planes):
            c, z, y_hi = s % 2, (s // 2) % rings, s // (2 * rings)
            x, y_lo = p // 2, p % 2
            z2, x2, y2 = move(c, z, x, 2 * y_hi + y_lo)
            y2 = y2 % 4
            s2 = ((y2 // 2) * rings + z2 % rings) * 2 + c
            pairs.append((s * planes + p, s2 * planes + (x2 % (planes // 2)) * 2 + y2 % 2))
    return pairs


def local(
    features,
    gain,
    w_query,
    w_key,
    w_value,
    w_out,
    w_face,
    gamma,
    positions,
    key_bias,
    block_mask,
    send_list,
    neighbour,
    cotangent,
):
    slabs, planes = lax.axis_size("slab"), lax.axis_size("plane")
    slab, plane = lax.axis_index("slab"), lax.axis_index("plane")
    core = slab % 2
    rings = slabs // 4
    x_at, y_at = plane // 2, (slab // (2 * rings)) * 2 + plane % 2

    def along(value, axis, target):
        return lax.ppermute(value, axis, [(i, target(i)) for i in range(lax.axis_size(axis))])

    def partner(value):
        return along(value, "slab", lambda s: s ^ 1)

    def near1(value):
        return along(value, "slab", lambda s: (s + 1 if s % 2 else s - 1) % slabs)

    def near2(value):
        return along(value, "slab", lambda s: (s - 2 if s % 2 else s + 2) % slabs)

    def near2_back(value):
        return along(value, "slab", lambda s: (s + 2 if s % 2 else s - 2) % slabs)

    def near3(value):
        return along(value, "slab", lambda s: (s + 3 if s % 2 else s - 3) % slabs)

    def opposite3(value):
        return along(value, "slab", lambda s: (s - 3 if s % 2 else s + 3) % slabs)

    def plane_pair(value):
        return along(value, "plane", lambda p: p ^ 1)

    def plane_cross(value):
        return along(value, "plane", lambda p: (p + 1 if p % 2 else p - 1) % planes)

    def outer_step(value, k):
        pairs = device_order(
            slabs, planes, lambda c, z, x, y: (z, x, y ^ k) if c else (z, x ^ k, y)
        )
        return lax.ppermute(value, BOTH, pairs)

    def inner_step(value, k):
        pairs = device_order(
            slabs, planes, lambda c, z, x, y: (z, x ^ k, y) if c else (z, x, y ^ k)
        )
        return lax.ppermute(value, BOTH, pairs)

    def z_flip(value, k):
        pairs = device_order(slabs, planes, lambda c, z, x, y: (z ^ k, x, y))
        return lax.ppermute(value, BOTH, pairs)

    tie = lax.optimization_barrier
    packed = shape((N + 16, D), BF)
    pack, face_pack = call(pack_kernel, (packed, packed), limit=60)(
        features, positions, key_bias, cotangent, neighbour[None]
    )
    cot_one = plane_pair(face_pack)
    cot_two = plane_cross(face_pack)
    fwd2 = opposite3(pack)
    got3 = near3(pack)
    got2 = near2(pack)
    fwd1 = near2_back(pack)
    cot_one, cot_two, near_pack = tie((cot_one, cot_two, pack))
    got1 = near1(near_pack)
    fwd0 = partner(near_pack)

    offsets = (1 - 2 * core) * jnp.array([0, -1, -2, -3, 1, 2, 3], jnp.int32)
    allow = block_mask[0, 0][(slab + offsets) % slabs]
    half = jnp.stack([core, plane % 2]).astype(jnp.int32)

    weight = pltpu.VMEM((D, D), BF)
    sides = (
        shape((N, D), BF),
        shape((N, D), BF),
        shape((N, D), BF),
        shape((N, D), F32),
        shape((D, N), F32),
        shape((3, D, N), BF),
        shape((D, N), F32),
        shape((D, N), F32),
        shape((D, N), BF),
    )
    results = call(
        attend_kernel,
        (shape((16, 80, D), BF), shape((16, 80, D), BF), *sides),
        scratch=(
            *([weight] * 5),
            pltpu.SemaphoreType.DMA((5,)),
            pltpu.VMEM((16, 80, D), BF),
            pltpu.VMEM((16, 80, D), BF),
            pltpu.SemaphoreType.DMA((5,)),
            pltpu.SemaphoreType.DMA((5,)),
            pltpu.VMEM((D, KEYS), BF),
            pltpu.VMEM((D, KEYS), BF),
            pltpu.VMEM((D, KEYS), BF),
            pltpu.VMEM((N, D), BF),
            pltpu.VMEM((2, D, N), BF),
            pltpu.VMEM((KEYS, D), BF),
            pltpu.VMEM((KEYS, D), BF),
            pltpu.VMEM((KEYS, D), BF),
            pltpu.VMEM((KEYS, N), BF),
            pltpu.VMEM((N, N), BF),
            pltpu.VMEM((N, D), BF),
            pltpu.VMEM((7, N + 16, D), BF),
            pltpu.VMEM((2, N + 16, D), BF),
            pltpu.VMEM((N, D), BF),
            pltpu.SemaphoreType.DMA((10,)),
            pltpu.SemaphoreType.DMA((9,)),
            *[pltpu.VMEM(side.shape, side.dtype) for side in sides],
        ),
        smem=4,
        flops=6000000000,
        limit=60,
        far=(*range(4, 14), *range(16, 21)),
        far_out=range(11),
    )(
        offsets,
        allow,
        gamma,
        half,
        pack,
        got1,
        got2,
        got3,
        fwd0,
        fwd1,
        fwd2,
        cotangent,
        cot_two,
        cot_one,
        send_list,
        gain[None],
        w_key,
        w_value,
        w_query,
        w_face,
        w_out,
    )
    send, keep, sent0, sent1, mixed, d_mixed = results[:6]
    dx_own, dx_part, dx_near1, dx_near2, dx_near3 = results[6:]
    got = partner(send)
    keep = hold(keep)

    outer_at = jnp.where(core == 0, x_at, y_at)
    inner_at = jnp.where(core == 0, y_at, x_at)
    place = jnp.stack([outer_at, inner_at, core]).astype(jnp.int32)
    order = (2, 1, 3)
    chunk = shape((4, 80, D), BF)
    first = call(split_kernel, (shape((4, 80, D), F32), chunk, chunk, chunk), smem=1)(
        place, keep, got
    )
    first, dx_part, dx_near3 = tie((first, dx_part, dx_near3))
    got_first = [outer_step(first[k], k) for k in order]
    back = partner(dx_part)
    back3 = near3(dx_near3)
    got_first, back, back3 = tie((got_first, back, back3))

    chunk = shape((80, D), BF)
    second = call(resplit_kernel, (shape((80, D), F32), chunk, chunk, chunk), smem=1)(
        place, first[0], *got_first
    )
    second, sent0, sent1 = tie((second, sent0, sent1))
    got_second = [inner_step(second[k], k) for k in order]
    face_one = plane_pair(sent0)
    face_two = plane_cross(sent1)
    got_second, face_one, face_two = tie((got_second, face_one, face_two))
    total = call(join_kernel, chunk)(second[0], *got_second)
    total = call(pair_kernel, chunk)(total, z_flip(total, 1))
    total, face_one, face_two = tie((total, face_one, face_two))
    near = z_flip(total, 2)
    out = call(out_kernel, shape((N, D), BF), smem=1)(
        half, neighbour[None], face_one, face_two, mixed, w_face
    )
    near, out = tie((near, out))
    total = call(pair_kernel, chunk)(total, near)
    total, dx_near1, dx_near2 = tie((total, dx_near1, dx_near2))
    near = z_flip(total, 4)
    to_one, to_two = call(add_kernel, (shape((D, N), BF),) * 2)(dx_near1, dx_near2, back)
    near, to_one, to_two = tie((near, to_one, to_two))
    total = call(pair_kernel, chunk)(total, near)

    total, meet = tie((total, partner(total)))
    inner = {0: total}
    for k in order:
        inner[k] = inner_step(total, k)
    block = jnp.stack([inner[k] for k in range(4)])
    block, to_one, to_two = tie((block, to_one, to_two))
    outer = {0: block}
    for k in order:
        outer[k] = outer_step(block, k)
    back1 = near1(to_one)
    back2 = near2_back(to_two)
    mine = [outer[k] for k in range(4)]
    d_input = call(input_kernel, shape((N, D), BF))(
        dx_own, back, back1, back2, back3, d_mixed, features, gain[None]
    )
    mine, d_input = tie((mine, d_input))
    other = partner(mine)
    grads = (shape((D, D), F32),) * 5
    scratch = (pltpu.VMEM((5, 256, D), F32), pltpu.SemaphoreType.DMA((5,)))
    every = tuple(range(5))
    grads = call(
        functools.partial(finish_kernel, 0), grads, scratch, smem=1, far=(5,), far_out=every
    )(place, *mine, meet)
    weights = call(
        functools.partial(finish_kernel, 1),
        (shape((D, D), F32),) * 5,
        scratch,
        smem=1,
        far=tuple(range(5, 10)),
        far_out=every,
        alias={5 + number: number for number in every},
    )(place, *other, *grads)
    d_out_w, d_face, d_query_w, d_key_w, d_value_w = weights

    return (out, d_input, d_query_w, d_key_w, d_value_w, d_out_w, d_face)


def solution(mesh):
    rows = P(BOTH, None)
    return jax.shard_map(
        local,
        mesh=mesh,
        in_specs=(
            rows,
            P(),
            P(),
            P(),
            P(),
            P(),
            P(),
            P(),
            P(None, BOTH),
            P(None, BOTH),
            P("plane", "slab", None),
            P(None, BOTH),
            P(BOTH),
            rows,
        ),
        out_specs=(rows, rows, P(), P(), P(), P(), P()),
        check_vma=False,
    )
```

```python
import functools

import jax
import jax.numpy as jnp
from jax import lax
from jax.experimental import pallas as pl
from jax.experimental.pallas import tpu as pltpu
from jax.sharding import PartitionSpec as P

EPS = 1e-06
BF = jnp.bfloat16
F32 = jnp.float32
BOTH = ("slab", "plane")
N = 128
D = 512
HEADS = 8
WINDOW = 7
KEYS = WINDOW * N


def dot(a, b, ca=1, cb=0):
    return lax.dot_general(a, b, (((ca,), (cb,)), ((), ())), preferred_element_type=F32)


def pieces(value):
    high = value.astype(BF).astype(F32)
    rest = value - high
    mid = rest.astype(BF).astype(F32)
    return high, mid, rest - mid


def half_grads(stage, target, sems, start, normed_t, dk_t, dv_t, left, dq, d_mixed_b, grad_rows):
    copies = []
    rows = normed_t[pl.ds(start, 256), :]
    for number in range(5):
        if number == 0:
            grad = dot(left[0, pl.ds(start, 256), :], d_mixed_b)
        elif number == 1:
            grad = dot(left[1, pl.ds(start, 256), :], grad_rows)
        elif number == 2:
            grad = dot(rows[:, 0:N], dq)
        else:
            grad = dot(rows, (dk_t if number == 3 else dv_t)[...], 1, 1)
        grad = grad.astype(BF)
        part = slice(number * 16, (number + 1) * 16)
        for chunk in range(16):
            stage[chunk, part, :] = grad[chunk * 16 : (chunk + 1) * 16]
        copy = pltpu.make_async_copy(stage.at[:, part, :], target.at[:, part, :], sems.at[number])
        copy.start()
        copies.append(copy)
    return copies


def attend_kernel(offs_ref, allow_ref, gamma_ref, half_ref, *refs):
    pack_hbm, refs = refs[:7], refs[7:]
    cot_hbm, refs = refs[:3], refs[3:]
    list_ref, gain_ref, refs = refs[0], refs[1], refs[2:]
    weight_hbm, refs = refs[:5], refs[5:]
    send_ref, keep_ref, refs = refs[0], refs[1], refs[2:]
    out_hbm, refs = refs[:9], refs[9:]
    wk_ref, wv_ref, wq_ref, wf_ref, wo_ref = weight_refs = refs[:5]
    weight_sems, send_stage, keep_stage, send_sems, keep_sems = refs[5:10]
    normed_t_ref, dk_t_ref, dv_t_ref, dq_ref, left_ref = refs[10:15]
    normed_ref, k_ref, v_ref, augk_ref, augq_ref, ho_ref = refs[15:21]
    packs, cot_pair, cot_ref, in_sems, out_sems = refs[21:26]
    stages = refs[26:]
    sent0_ref, sent1_ref, mixed_ref, dmix_ref, dx_own_ref = stages[:5]
    dx_part_ref, dx_near1_ref, dx_near2_ref, dx_near3_ref = stages[5:]

    arrivals = []
    for number, source in enumerate(pack_hbm):
        copy = pltpu.make_async_copy(source, packs.at[number], in_sems.at[number])
        copy.start()
        arrivals.append(copy)
    loads = []
    for number, (source, target) in enumerate(zip(weight_hbm, weight_refs)):
        load = pltpu.make_async_copy(source, target, weight_sems.at[number])
        load.start()
        loads.append(load)
    cot_targets = (cot_ref, cot_pair.at[0], cot_pair.at[1])
    for number, (source, target) in enumerate(zip(cot_hbm, cot_targets)):
        load = pltpu.make_async_copy(source, target, in_sems.at[7 + number])
        load.start()
        loads.append(load)
    copies = []

    def flush(*numbers):
        for number in numbers:
            copy = pltpu.make_async_copy(stages[number], out_hbm[number], out_sems.at[number])
            copy.start()
            copies.append(copy)

    gain = gain_ref[...]
    row16 = lax.broadcasted_iota(jnp.int32, (HEADS, 16, N), 1)
    axis = jnp.where(row16 < 12, row16 // 3, 4)
    gam = jnp.concatenate([jnp.full((1, 1), gamma_ref[h], F32) for h in range(HEADS)], axis=0)
    for number in range(7):
        arrivals[number].wait()
        rows = slice(number * N, (number + 1) * N)
        x = packs[number, 0:N, :].astype(F32)
        inverse = lax.rsqrt(jnp.mean(x * x, axis=1, keepdims=True) + EPS)
        normed = (x * inverse * gain).astype(BF)
        normed_ref[rows, :] = normed
        normed_t_ref[:, rows] = normed.T
        small = packs[number, N : N + 16, 0:N].astype(F32)
        offset = offs_ref[number].astype(F32)
        px, py, pz = small[0:1], small[1:2], small[2:3]
        lifted = pz + offset
        norm2 = px * px + py * py + lifted * lifted
        bias = small[3:11] - gam * norm2
        bias = jnp.where(allow_ref[number] > 0, bias, -1e30)
        high, mid, low = pieces(bias)
        points = (px[None], py[None], pz[None])
        aug = jnp.where(axis == 3, offset, 0.0)
        for which, point in enumerate(points):
            aug = jnp.where(axis == which, point, aug)
        for which, piece in enumerate((high, mid, low)):
            aug = jnp.where(row16 == 12 + which, piece[:, None, :], aug)
        augk_ref[rows, :] = aug.reshape(N, N).T.astype(BF)
        if number == 0:
            aug = jnp.where(axis == 0, points[0], jnp.where(axis == 1, points[1], points[2]))
            high, mid, low = pieces(aug * (2.0 * gam[:, :, None]))
            aug = jnp.where(row16 % 3 == 0, high, jnp.where(row16 % 3 == 1, mid, low))
            aug = jnp.where(row16 < 12, aug, jnp.where(row16 < 15, 1.0, 0.0))
            augq_ref[...] = aug.reshape(N, N).T.astype(BF)

    loads[0].wait()
    loads[1].wait()
    k_ref[...] = dot(normed_ref[...], wk_ref[...]).astype(BF)
    v_ref[...] = dot(normed_ref[...], wv_ref[...]).astype(BF)
    for load in loads[2:]:
        load.wait()
    query = (dot(normed_ref[0:N, :], wq_ref[...]).astype(BF) * 0.125).astype(BF)

    row_n = lax.broadcasted_iota(jnp.int32, (N, N), 0)
    list0 = jnp.where(row_n == list_ref[0:1, :], 1.0, 0.0).astype(BF)
    list1 = jnp.where(row_n == list_ref[1:2, :], 1.0, 0.0).astype(BF)
    row_f = row_n.astype(F32)
    even = half_ref[1] == 0
    cot_two, cot_one = cot_pair[0], cot_pair[1]
    cot_up = jnp.where(even, cot_one, cot_two)
    cot_dn = jnp.where(even, cot_two, cot_one)
    near_up = cot_up[N : N + 16, 0:N].astype(F32)[0:1]
    near_dn = cot_dn[N : N + 16, 0:N].astype(F32)[0:1]
    pick_up = jnp.where(row_f == near_up, 1.0, 0.0).astype(BF)
    pick_dn = jnp.where(row_f + 128.0 == near_dn, 1.0, 0.0).astype(BF)
    grad_rows = dot(dot(list1, pick_up).astype(BF), cot_up[0:N, :])
    grad_rows = grad_rows + dot(dot(list0, pick_dn).astype(BF), cot_dn[0:N, :])
    grad_rows = grad_rows.astype(BF)
    d_mixed = cot_ref[...].astype(F32) + dot(grad_rows, wf_ref[...], 1, 1)
    dmix_ref[...] = d_mixed
    flush(3)
    d_mixed_b = d_mixed.astype(BF)
    d_heads = dot(d_mixed_b, wo_ref[...], 1, 1).astype(BF)

    lane = lax.broadcasted_iota(jnp.int32, (N, N), 1)
    first = lane < 64
    masks = (first, jnp.logical_not(first))
    masks_b = tuple(jnp.where(m, 1.0, 0.0).astype(BF) for m in masks)
    for pair in range(HEADS // 2):
        cols = slice(pair * N, (pair + 1) * N)
        keys = k_ref[:, cols]
        values = v_ref[:, cols]
        keys_aug = jnp.concatenate([keys, augk_ref[...]], axis=1)
        qp = query[:, cols]
        gp = d_heads[:, cols]
        q_parts = [qp * m for m in masks_b]
        g_parts = [gp * m for m in masks_b]
        shares = []
        probs = []
        probs_b = []
        outs = []
        for t in range(2):
            h = 2 * pair + t
            mine = jnp.where(lane // 16 == h, 1.0, 0.0).astype(BF)
            left = jnp.concatenate([q_parts[t], augq_ref[...] * mine], axis=1)
            scores = dot(left, keys_aug, 1, 1)
            top = jnp.max(scores, axis=1, keepdims=True)
            weights = jnp.exp(scores - top)
            shares.append(1.0 / jnp.sum(weights, axis=1, keepdims=True))
            probs.append(weights)
            probs_b.append(weights.astype(BF))
            outs.append(dot(probs_b[t], values) * shares[t])
        merged = jnp.where(first, outs[0], outs[1]).astype(BF)
        ho_ref[:, cols] = merged
        inner = gp.astype(F32) * merged.astype(F32)
        scores_b = []
        dqs = []
        for t in range(2):
            delta = jnp.sum(jnp.where(masks[t], inner, 0.0), axis=1, keepdims=True)
            d_prob = dot(g_parts[t], values, 1, 1)
            d_score = (probs[t] * (d_prob - delta)).astype(BF)
            scores_b.append(d_score)
            dqs.append(dot(d_score, keys) * shares[t])
        dq_ref[:, cols] = (jnp.where(first, dqs[0], dqs[1]) * 0.125).astype(BF)
        q_parts = [(q.astype(F32) * share).astype(BF) for q, share in zip(q_parts, shares)]
        g_parts = [(g.astype(F32) * share).astype(BF) for g, share in zip(g_parts, shares)]
        dk_t_ref[cols, :] = dot(
            jnp.concatenate(q_parts, axis=0), jnp.concatenate(scores_b, axis=0), 0, 0
        ).astype(BF)
        dv_t_ref[cols, :] = dot(
            jnp.concatenate(g_parts, axis=0), jnp.concatenate(probs_b, axis=0), 0, 0
        ).astype(BF)

    heads_out = ho_ref[...]
    mixed = (packs[0, 0:N, :].astype(F32) + dot(heads_out, wo_ref[...])).astype(BF)
    mixed_ref[...] = mixed
    sent0_ref[...] = dot(jnp.where(even, list1, list0), mixed, 0, 0).astype(BF)
    sent1_ref[...] = dot(jnp.where(even, list0, list1), mixed, 0, 0).astype(BF)
    flush(0, 1, 2)
    dq = dq_ref[...]
    dx_t = dot(wk_ref[...], dk_t_ref[...]) + dot(wv_ref[...], dv_t_ref[...])
    dx_own_ref[...] = dx_t[:, 0:N] + dot(wq_ref[...], dq, 1, 1)
    dx_near1_ref[...] = dx_t[:, N : 2 * N]
    dx_near2_ref[...] = dx_t[:, 2 * N : 3 * N]
    dx_near3_ref[...] = dx_t[:, 3 * N : 4 * N].astype(BF)
    for number in range(3):
        first = (4 + number) * N
        dx_part_ref[number] = dx_t[:, first : first + N].astype(BF)
    flush(4, 5, 6, 7, 8)

    left_ref[0] = heads_out.T
    left_ref[1] = mixed.T
    mine = half_ref[0]
    for stage, target, sems, side in (
        (send_stage, send_ref, send_sems, 1 - mine),
        (keep_stage, keep_ref, keep_sems, mine),
    ):
        copies += half_grads(
            stage,
            target,
            sems,
            pl.multiple_of(side * 256, 256),
            normed_t_ref,
            dk_t_ref,
            dv_t_ref,
            left_ref,
            dq,
            d_mixed_b,
            grad_rows,
        )

    for copy in copies:
        copy.wait()


def shape(dims, kind):
    return jax.ShapeDtypeStruct(dims, kind)


def whole(dims):
    return pl.BlockSpec(dims, lambda i: (0,) * len(dims), pipeline_mode=pl.Buffered(1))


def call(kernel, outs, scratch=(), smem=0, flops=1000000, limit=16, far=(), far_out=(), alias=None):
    single = not isinstance(outs, tuple)
    outs = (outs,) if single else outs

    def run(*args):
        hbm = pl.BlockSpec(memory_space=pl.ANY)
        specs = [
            pl.BlockSpec(memory_space=pltpu.SMEM) if number < smem else whole(arg.shape)
            for number, arg in enumerate(args)
        ]
        for number in far:
            specs[number] = hbm
        out_specs = [
            hbm if number in far_out else whole(out.shape) for number, out in enumerate(outs)
        ]
        results = pl.pallas_call(
            kernel,
            grid=(1,),
            out_shape=outs,
            in_specs=specs,
            out_specs=out_specs,
            input_output_aliases=alias or {},
            scratch_shapes=list(scratch),
            compiler_params=pltpu.CompilerParams(vmem_limit_bytes=limit * 1024 * 1024),
            cost_estimate=pl.CostEstimate(
                flops=flops, bytes_accessed=4000000, transcendentals=0
            ),
        )(*args)
        return results[0] if single else results

    return run


def pack_kernel(x_ref, pos_ref, bias_ref, cot_ref, near_ref, pack_ref, face_ref):
    pack_ref[0:N, :] = x_ref[...]
    face_ref[0:N, :] = cot_ref[...]
    zeros = jnp.zeros((16, D - N), BF)
    small = jnp.concatenate(
        [pos_ref[...].astype(F32), bias_ref[...].astype(F32), jnp.zeros((5, N), F32)], axis=0
    )
    pack_ref[N : N + 16, :] = jnp.concatenate([small.astype(BF), zeros], axis=1)
    near = jnp.broadcast_to(near_ref[...].astype(F32), (16, N)).astype(BF)
    face_ref[N : N + 16, :] = jnp.concatenate([near, zeros], axis=1)


def hold_kernel(keep_ref, out_ref, sem):
    copy = pltpu.make_async_copy(keep_ref, out_ref, sem)
    copy.start()
    copy.wait()


def hold(value):
    return pl.pallas_call(
        hold_kernel,
        out_shape=shape(value.shape, value.dtype),
        in_specs=[pl.BlockSpec(memory_space=pl.ANY)],
        out_specs=pl.BlockSpec(memory_space=pltpu.VMEM),
        scratch_shapes=[pltpu.SemaphoreType.DMA],
        compiler_params=pltpu.CompilerParams(vmem_limit_bytes=8 * 1024 * 1024),
        cost_estimate=pl.CostEstimate(
            flops=1000000000, bytes_accessed=4000000, transcendentals=0
        ),
    )(value)


def split_kernel(place_ref, keep_ref, recv_ref, *outs):
    for step, out in enumerate(outs):
        rows = pl.ds((place_ref[0] ^ step) * 4, 4)
        total = keep_ref[rows].astype(F32) + recv_ref[rows].astype(F32)
        out[...] = total.astype(out.dtype)


def resplit_kernel(place_ref, own_ref, a_ref, b_ref, c_ref, *outs):
    for step, out in enumerate(outs):
        chunk = place_ref[1] ^ step
        total = own_ref[chunk] + a_ref[chunk].astype(F32)
        total = total + b_ref[chunk].astype(F32) + c_ref[chunk].astype(F32)
        out[...] = total.astype(out.dtype)


def join_kernel(own_ref, a_ref, b_ref, c_ref, out_ref):
    total = own_ref[...] + a_ref[...].astype(F32)
    out_ref[...] = (total + b_ref[...].astype(F32) + c_ref[...].astype(F32)).astype(BF)


def pair_kernel(a_ref, b_ref, out_ref):
    out_ref[...] = (a_ref[...].astype(F32) + b_ref[...].astype(F32)).astype(BF)


def finish_kernel(whose, place_ref, *refs):
    parts, refs = refs[:4], refs[5 + 4 * whose :]
    outs, stage, sems = refs[:5], refs[5], refs[6]
    core = place_ref[2]
    side = core if whose == 0 else 1 - core
    copies = []
    for number in range(5):
        rows = slice(number * 16, (number + 1) * 16)
        for big in range(4):
            outer = place_ref[whose] ^ big
            for little in range(4):
                inner = place_ref[1 - whose] ^ little
                start = pl.multiple_of(outer * 64 + inner * 16, 16)
                piece = parts[big][little, rows, :]
                stage[number, pl.ds(start, 16), :] = piece.astype(F32)
        target = outs[number].at[pl.ds(pl.multiple_of(side * 256, 256), 256), :]
        copy = pltpu.make_async_copy(stage.at[number], target, sems.at[number])
        copy.start()
        copies.append(copy)
    for copy in copies:
        copy.wait()


def out_kernel(parity_ref, near_ref, one_ref, two_ref, mixed_ref, wf_ref, out_ref):
    even = parity_ref[1] == 0
    one, two = one_ref[...], two_ref[...]
    row = lax.broadcasted_iota(jnp.int32, (2 * N, N), 0)
    pick = jnp.where(row == near_ref[...], 1.0, 0.0).astype(BF)
    received = jnp.concatenate([jnp.where(even, two, one), jnp.where(even, one, two)], axis=0)
    picked = dot(pick, received, 0, 0).astype(BF)
    out_ref[...] = (mixed_ref[...].astype(F32) + dot(picked, wf_ref[...])).astype(BF)


def add_kernel(one_ref, two_ref, recv_ref, to_one_ref, to_two_ref):
    to_one_ref[...] = (one_ref[...] + recv_ref[1].astype(F32)).astype(BF)
    to_two_ref[...] = (two_ref[...] + recv_ref[2].astype(F32)).astype(BF)


def input_kernel(own_ref, *refs):
    parts, (dmix_ref, x_ref, gain_ref, out_ref) = refs[:4], refs[4:]
    total = own_ref[...]
    for part in parts:
        total = total + (part[0] if len(part.shape) == 3 else part[...]).astype(F32)
    scaled = gain_ref[...] * total.T
    x = x_ref[...].astype(F32)
    inverse = lax.rsqrt(jnp.mean(x * x, axis=1, keepdims=True) + EPS)
    drop = x * (inverse * inverse * inverse) * jnp.mean(scaled * x, axis=1, keepdims=True)
    out_ref[...] = (dmix_ref[...] + inverse * scaled - drop).astype(BF)


def device_order(slabs, planes, move):
    rings = slabs // 4
    pairs = []
    for s in range(slabs):
        for p in range(planes):
            c, z, y_hi = s % 2, (s // 2) % rings, s // (2 * rings)
            x, y_lo = p // 2, p % 2
            z2, x2, y2 = move(c, z, x, 2 * y_hi + y_lo)
            y2 = y2 % 4
            s2 = ((y2 // 2) * rings + z2 % rings) * 2 + c
            pairs.append((s * planes + p, s2 * planes + (x2 % (planes // 2)) * 2 + y2 % 2))
    return pairs


def local(
    features,
    gain,
    w_query,
    w_key,
    w_value,
    w_out,
    w_face,
    gamma,
    positions,
    key_bias,
    block_mask,
    send_list,
    neighbour,
    cotangent,
):
    slabs, planes = lax.axis_size("slab"), lax.axis_size("plane")
    slab, plane = lax.axis_index("slab"), lax.axis_index("plane")
    core = slab % 2
    rings = slabs // 4
    x_at, y_at = plane // 2, (slab // (2 * rings)) * 2 + plane % 2

    def along(value, axis, target):
        return lax.ppermute(value, axis, [(i, target(i)) for i in range(lax.axis_size(axis))])

    def partner(value):
        return along(value, "slab", lambda s: s ^ 1)

    def near1(value):
        return along(value, "slab", lambda s: (s + 1 if s % 2 else s - 1) % slabs)

    def near2(value):
        return along(value, "slab", lambda s: (s - 2 if s % 2 else s + 2) % slabs)

    def near2_back(value):
        return along(value, "slab", lambda s: (s + 2 if s % 2 else s - 2) % slabs)

    def near3(value):
        return along(value, "slab", lambda s: (s + 3 if s % 2 else s - 3) % slabs)

    def opposite3(value):
        return along(value, "slab", lambda s: (s - 3 if s % 2 else s + 3) % slabs)

    def plane_pair(value):
        return along(value, "plane", lambda p: p ^ 1)

    def plane_cross(value):
        return along(value, "plane", lambda p: (p + 1 if p % 2 else p - 1) % planes)

    def outer_step(value, k):
        pairs = device_order(
            slabs, planes, lambda c, z, x, y: (z, x, y ^ k) if c else (z, x ^ k, y)
        )
        return lax.ppermute(value, BOTH, pairs)

    def inner_step(value, k):
        pairs = device_order(
            slabs, planes, lambda c, z, x, y: (z, x ^ k, y) if c else (z, x, y ^ k)
        )
        return lax.ppermute(value, BOTH, pairs)

    def z_flip(value, k):
        pairs = device_order(slabs, planes, lambda c, z, x, y: (z ^ k, x, y))
        return lax.ppermute(value, BOTH, pairs)

    tie = lax.optimization_barrier
    packed = shape((N + 16, D), BF)
    pack, face_pack = call(pack_kernel, (packed, packed), limit=60)(
        features, positions, key_bias, cotangent, neighbour[None]
    )
    cot_one = plane_pair(face_pack)
    cot_two = plane_cross(face_pack)
    fwd2 = opposite3(pack)
    got3 = near3(pack)
    got2 = near2(pack)
    fwd1 = near2_back(pack)
    cot_one, cot_two, near_pack = tie((cot_one, cot_two, pack))
    got1 = near1(near_pack)
    fwd0 = partner(near_pack)

    offsets = (1 - 2 * core) * jnp.array([0, -1, -2, -3, 1, 2, 3], jnp.int32)
    allow = block_mask[0, 0][(slab + offsets) % slabs]
    half = jnp.stack([core, plane % 2]).astype(jnp.int32)

    weight = pltpu.VMEM((D, D), BF)
    sides = (
        shape((N, D), BF),
        shape((N, D), BF),
        shape((N, D), BF),
        shape((N, D), F32),
        shape((D, N), F32),
        shape((3, D, N), BF),
        shape((D, N), F32),
        shape((D, N), F32),
        shape((D, N), BF),
    )
    results = call(
        attend_kernel,
        (shape((16, 80, D), BF), shape((16, 80, D), BF), *sides),
        scratch=(
            *([weight] * 5),
            pltpu.SemaphoreType.DMA((5,)),
            pltpu.VMEM((16, 80, D), BF),
            pltpu.VMEM((16, 80, D), BF),
            pltpu.SemaphoreType.DMA((5,)),
            pltpu.SemaphoreType.DMA((5,)),
            pltpu.VMEM((D, KEYS), BF),
            pltpu.VMEM((D, KEYS), BF),
            pltpu.VMEM((D, KEYS), BF),
            pltpu.VMEM((N, D), BF),
            pltpu.VMEM((2, D, N), BF),
            pltpu.VMEM((KEYS, D), BF),
            pltpu.VMEM((KEYS, D), BF),
            pltpu.VMEM((KEYS, D), BF),
            pltpu.VMEM((KEYS, N), BF),
            pltpu.VMEM((N, N), BF),
            pltpu.VMEM((N, D), BF),
            pltpu.VMEM((7, N + 16, D), BF),
            pltpu.VMEM((2, N + 16, D), BF),
            pltpu.VMEM((N, D), BF),
            pltpu.SemaphoreType.DMA((10,)),
            pltpu.SemaphoreType.DMA((9,)),
            *[pltpu.VMEM(side.shape, side.dtype) for side in sides],
        ),
        smem=4,
        flops=6000000000,
        limit=60,
        far=(*range(4, 14), *range(16, 21)),
        far_out=range(11),
    )(
        offsets,
        allow,
        gamma,
        half,
        pack,
        got1,
        got2,
        got3,
        fwd0,
        fwd1,
        fwd2,
        cotangent,
        cot_two,
        cot_one,
        send_list,
        gain[None],
        w_key,
        w_value,
        w_query,
        w_face,
        w_out,
    )
    send, keep, sent0, sent1, mixed, d_mixed = results[:6]
    dx_own, dx_part, dx_near1, dx_near2, dx_near3 = results[6:]
    got = partner(send)
    keep = hold(keep)

    outer_at = jnp.where(core == 0, x_at, y_at)
    inner_at = jnp.where(core == 0, y_at, x_at)
    place = jnp.stack([outer_at, inner_at, core]).astype(jnp.int32)
    order = (2, 1, 3)
    chunk = shape((4, 80, D), BF)
    first = call(split_kernel, (shape((4, 80, D), F32), chunk, chunk, chunk), smem=1)(
        place, keep, got
    )
    first, dx_part, dx_near3 = tie((first, dx_part, dx_near3))
    got_first = [outer_step(first[k], k) for k in order]
    back = partner(dx_part)
    back3 = near3(dx_near3)
    got_first, back, back3 = tie((got_first, back, back3))

    chunk = shape((80, D), BF)
    second = call(resplit_kernel, (shape((80, D), F32), chunk, chunk, chunk), smem=1)(
        place, first[0], *got_first
    )
    second, sent0, sent1 = tie((second, sent0, sent1))
    got_second = [inner_step(second[k], k) for k in order]
    face_one = plane_pair(sent0)
    face_two = plane_cross(sent1)
    got_second, face_one, face_two = tie((got_second, face_one, face_two))
    total = call(join_kernel, chunk)(second[0], *got_second)
    total = call(pair_kernel, chunk)(total, z_flip(total, 1))
    total, face_one, face_two = tie((total, face_one, face_two))
    near = z_flip(total, 2)
    out = call(out_kernel, shape((N, D), BF), smem=1)(
        half, neighbour[None], face_one, face_two, mixed, w_face
    )
    near, out = tie((near, out))
    total = call(pair_kernel, chunk)(total, near)
    total, dx_near1, dx_near2 = tie((total, dx_near1, dx_near2))
    near = z_flip(total, 4)
    to_one, to_two = call(add_kernel, (shape((D, N), BF),) * 2)(dx_near1, dx_near2, back)
    near, to_one, to_two = tie((near, to_one, to_two))
    total = call(pair_kernel, chunk)(total, near)

    total, meet = tie((total, partner(total)))
    inner = {0: total}
    for k in order:
        inner[k] = inner_step(total, k)
    block = jnp.stack([inner[k] for k in range(4)])
    block, to_one, to_two = tie((block, to_one, to_two))
    outer = {0: block}
    for k in order:
        outer[k] = outer_step(block, k)
    back1 = near1(to_one)
    back2 = near2_back(to_two)
    mine = [outer[k] for k in range(4)]
    d_input = call(input_kernel, shape((N, D), BF))(
        dx_own, back, back1, back2, back3, d_mixed, features, gain[None]
    )
    mine, d_input = tie((mine, d_input))
    other = partner(mine)
    grads = (shape((D, D), F32),) * 5
    scratch = (pltpu.VMEM((5, 256, D), F32), pltpu.SemaphoreType.DMA((5,)))
    every = tuple(range(5))
    grads = call(
        functools.partial(finish_kernel, 0), grads, scratch, smem=1, far=(5,), far_out=every
    )(place, *mine, meet)
    weights = call(
        functools.partial(finish_kernel, 1),
        (shape((D, D), F32),) * 5,
        scratch,
        smem=1,
        far=tuple(range(5, 10)),
        far_out=every,
        alias={5 + number: number for number in every},
    )(place, *other, *grads)
    d_out_w, d_face, d_query_w, d_key_w, d_value_w = weights

    return (out, d_input, d_query_w, d_key_w, d_value_w, d_out_w, d_face)


def solution(mesh):
    rows = P(BOTH, None)
    return jax.shard_map(
        local,
        mesh=mesh,
        in_specs=(
            rows,
            P(),
            P(),
            P(),
            P(),
            P(),
            P(),
            P(),
            P(None, BOTH),
            P(None, BOTH),
            P("plane", "slab", None),
            P(None, BOTH),
            P(BOTH),
            rows,
        ),
        out_specs=(rows, rows, P(), P(), P(), P(), P()),
        check_vma=False,
    )
```
